128 devices in a mesh: front: 1, row: 64 (over z, y, x), col: 2 (over core).
Axes of the slice: x: 4, y: 4, z: 4, core: 2. Of those that a mesh axis runs over, the one named last changes fastest.
Arguments:
- contributions: float32 [64, 128, 4096], P(('front', 'row'), None, 'col'), may hold values from -0.088388348 to 0.088388348
- valid_rows: int32 [64], P(('front', 'row')), may hold values from 1 to 128, 5120 in all
Outputs:
- r_rows: float32 [512, 4096], P('front', 'col')
The draws below stay inside these ranges and needn't reach their ends.
All inputs are finite; a program needn't handle non-finite values. No bound on the sum of `valid_rows` on one device may be relied on, other than what follows from the above.
Results may differ from the reference program's by a relative error of at most 0.0003.
Values sent between devices are 32-bit elements; how exact they have to be, the bound alone decides.
No kernel may reach another device: no remote copies, remote signals or barrier semaphores. Data moves between devices by JAX's collectives and lax.ppermute only.
A program may use at most 64 MiB of HBM per device.

```python
import math
import jax
import jax.numpy as jnp
import numpy as np
from jax import lax

W = 4096
PANEL = 256
NPANEL = 2
BLOCK = 128
NBLK = 64


def draw_contributions(key, part):
    full_shape = (NBLK, BLOCK, W)
    spread = 1.0 / math.sqrt(BLOCK * NBLK)
    base_key = jax.random.fold_in(jax.random.fold_in(key, 11), 0)
    block_pos = jnp.arange(NBLK, dtype=jnp.float32) / max(NBLK - 1, 1)
    base_draw = jnp.clip(jax.random.normal(base_key, full_shape, jnp.float32), -4.0, 4.0)
    block_scale = jnp.exp(math.log(3.0) * (block_pos - 1.0))
    leading = NPANEL * PANEL
    column_ids = jnp.arange(W, dtype=jnp.int32)
    shifted = jnp.concatenate([jnp.zeros((NBLK, BLOCK, 1), jnp.float32), base_draw[:, :, :-1]], axis=2)
    mixing = 0.5 * ((column_ids >= 1) & (column_ids < leading)).astype(jnp.float32)
    mixed_cols = (base_draw + mixing[None, None, :] * shifted) * block_scale[:, None, None] * spread
    return jnp.clip(mixed_cols, -8.0 * spread, 8.0 * spread)


def split_up(number_of, total, most, slope):
    portions = [(1 << 20) // math.isqrt(rank ** slope) + 1 for rank in range(2, number_of + 1)]
    surplus, counts = total - most - (number_of - 1), [1] * (number_of - 1)
    while surplus > 0:
        movable = [i for i in range(number_of - 1) if counts[i] < most]
        pool, remaining = sum([portions[i] for i in movable]), surplus
        for i in movable:
            more = min(most - counts[i], max(1, remaining * portions[i] // pool), surplus)
            counts[i] = counts[i] + more
            surplus = surplus - more
    return np.array([most] + counts)


def uneven(own_key, number_of, total, reach, slope):
    if number_of == 2:
        one = jax.random.randint(own_key, (), max(1, total - reach), min(reach, total - 1) + 1)
        return jnp.stack([one, total - one])
    tallies = jnp.asarray(split_up(number_of, total, reach, slope), jnp.int32)
    couples = (number_of - 1) // 2
    giver, sink = tallies[1:1 + 2 * couples:2], tallies[2:2 + 2 * couples:2]
    slack = jnp.minimum(giver - 1, reach - sink)
    moved = jax.random.randint(jax.random.fold_in(own_key, 1), (couples,), 0, 1 << 20) % (slack + 1)
    tallies = tallies.at[1:1 + 2 * couples:2].set(giver - moved).at[2:2 + 2 * couples:2].set(sink + moved)
    return tallies[jax.random.permutation(jax.random.fold_in(own_key, 2), number_of)]


def setup_inputs(seed: int = 0, part: int = 0) -> dict:
    key_of = jax.random.split(jax.random.key(seed), 3)
    part_keys = jax.random.split(jax.random.fold_in(key_of[2], part), 3)
    return {
        "contributions": draw_contributions(jax.random.fold_in(jax.random.fold_in(key_of[2], part), 71), part),
        "valid_rows": uneven(part_keys[1], NBLK, NBLK * 80, BLOCK, 2).astype(jnp.int32),
    }


def reference(contributions, valid_rows):
    blocks, height, width = contributions.shape
    live_rows = (jnp.arange(height, dtype=jnp.int32)[None, :] < valid_rows[:, None]).astype(jnp.float32)
    frontal = (contributions * live_rows[:, :, None]).reshape(blocks * height, width)
    leading = NPANEL * PANEL
    basis, triangle = jnp.linalg.qr(frontal[:, :leading])
    sign_fix = jnp.sign(jnp.diagonal(triangle))
    projected = jnp.dot(basis.T, frontal, precision=lax.Precision.HIGHEST) * sign_fix[:, None]
    kept_mask = jnp.arange(width, dtype=jnp.int32)[None, :] >= jnp.arange(leading, dtype=jnp.int32)[:, None]
    return jnp.where(kept_mask, projected, jnp.zeros_like(projected))
```

```python
import jax
import jax.numpy as jnp
from jax import lax
from jax.sharding import PartitionSpec as P

LEAD = 512
HI = lax.Precision.HIGHEST


def body(contributions, valid_rows):
    blocks, height, width = contributions.shape
    live = jnp.arange(height, dtype=jnp.int32)[None, :] < valid_rows[:, None]
    frontal = jnp.where(live[:, :, None], contributions, 0.0).reshape(blocks * height, width)
    own = frontal[:, :LEAD]
    core = lax.axis_index("col")
    other = lax.ppermute(own, "col", [(0, 1), (1, 0)])
    lead = jnp.where(core == 0, own, other)
    gram = jnp.einsum("rp,rc->pc", lead, frontal, precision=HI)
    pieces = lax.all_to_all(gram.reshape(64, LEAD // 64, width), "row", 0, 0)
    mine = jnp.sum(pieces, axis=0)
    mine11 = mine[:, :LEAD]
    other11 = lax.ppermute(mine11, "col", [(0, 1), (1, 0)])
    mine11 = jnp.where(core == 0, mine11, other11)
    g11 = lax.all_to_all(jnp.broadcast_to(mine11[None], (64, LEAD // 64, LEAD)), "row", 0, 0)
    g11 = g11.reshape(LEAD, LEAD)
    mine, _ = lax.optimization_barrier((mine, g11[:8, :128]))
    gram_all = lax.all_gather(mine, "row", axis=0, tiled=True)
    factor = jnp.linalg.cholesky(g11, symmetrize_input=False)
    inverse = jax.scipy.linalg.solve_triangular(factor, jnp.eye(LEAD, dtype=jnp.float32), lower=True)
    projected = jnp.dot(inverse, gram_all, precision=HI)
    column_ids = core * width + jnp.arange(width, dtype=jnp.int32)
    kept = column_ids[None, :] >= jnp.arange(LEAD, dtype=jnp.int32)[:, None]
    return jnp.where(kept, projected, 0.0)


def solution(mesh):
    return jax.shard_map(
        body,
        mesh=mesh,
        in_specs=(P(("front", "row"), None, "col"), P(("front", "row"))),
        out_specs=P("front", "col"),
        check_vma=False,
    )
```

```python
import jax
import jax.numpy as jnp
from jax import lax
from jax.experimental import pallas as pl
from jax.experimental.pallas import tpu as pltpu
from jax.sharding import PartitionSpec as P

LEAD = 512
HI = lax.Precision.HIGHEST

S8=(8,128)
def lb(x,c): return jnp.broadcast_to(x[:,c:c+1],S8)
def sb(x,j): return jnp.broadcast_to(x[j:j+1,:],S8)

def chol_inv_128(V, sub, lane):
    V=list(V)
    E=[jnp.where(lane==sub+8*k,1.0,0.0) for k in range(16)]
    out=[]
    for k in range(16):
        X=V[k]
        LB=[lb(X,8*k+j) for j in range(8)]
        S=[[sb(LB[j],i) if i>=j else None for j in range(8)] for i in range(8)]
        R=[sb(X,j) for j in range(8)]
        F=[sb(E[k],j) for j in range(8)]
        l=[[None]*8 for _ in range(8)]
        inv=[None]*8
        for j in range(8):
            inv[j]=1.0/S[j][j]
            for i in range(j+1,8):
                l[i][j]=S[i][j]*inv[j]
                for m in range(j+1,i+1):
                    S[i][m]=S[i][m]-l[i][j]*S[m][j]
            for i in range(j+1,8):
                R[i]=R[i]-l[i][j]*R[j]
                F[i]=F[i]-l[i][j]*F[j]
        o=F[0]*lax.rsqrt(S[0][0])
        for j in range(1,8):
            o=jnp.where(sub==j,F[j]*lax.rsqrt(S[j][j]),o)
        out.append(o)
        if k<15:
            W=[R[j]*inv[j] for j in range(8)]
            H=[F[j]*inv[j] for j in range(8)]
            for i in range(7,0,-1):
                for j in range(i):
                    W[j]=W[j]-l[i][j]*W[i]
                    H[j]=H[j]-l[i][j]*H[i]
            for m in range(k+1,16):
                Y=V[m]; v=Y; e=E[m]
                for j in range(7,-1,-1):
                    c=lb(Y,8*k+j)
                    v=v-c*W[j]
                    e=e-c*H[j]
                V[m]=v; E[m]=e
    return out

def kernel(g_ref, o_ref, a, u, stack):
    a[...]=g_ref[...]
    o_ref[...]=jnp.zeros_like(o_ref)
    sub=lax.broadcasted_iota(jnp.int32,S8,0); lane=lax.broadcasted_iota(jnp.int32,S8,1)
    d=stack
    d[...]=g_ref[0:128,0:128]
    T=(((0,),(0,)),((),()))
    @pl.loop(0,4)
    def _(p):
        o=chol_inv_128([d[8*k:8*k+8,:] for k in range(16)],sub,lane)
        for k in range(16): d[8*k:8*k+8,:]=o[k]
        for q in range(4):
            @pl.when(p==q)
            def _():
                lo,hi=128*q,128*(q+1)
                linv=d[...]
                if q<3:
                    up=jnp.dot(linv,a[lo:hi,hi:],precision=HI,preferred_element_type=jnp.float32)
                    d[...]=a[hi:hi+128,hi:hi+128]-lax.dot_general(up[:,:128],up[:,:128],T,precision=HI,preferred_element_type=jnp.float32)
                    if q<2:
                        a[hi:,hi:]=a[hi:,hi:]-lax.dot_general(up,up,T,precision=HI,preferred_element_type=jnp.float32)
                o_ref[lo:hi,lo:hi]=linv
                if q>0:
                    o_ref[lo:hi,:lo]=jnp.dot(linv,o_ref[lo:hi,:lo],precision=HI,preferred_element_type=jnp.float32)
                if q<3:
                    o_ref[hi:,:hi]=o_ref[hi:,:hi]-lax.dot_general(up,o_ref[lo:hi,:hi],T,precision=HI,preferred_element_type=jnp.float32)

def inverse_factor(g):
    n=g.shape[0]
    return pl.pallas_call(kernel,out_shape=jax.ShapeDtypeStruct((n,n),jnp.float32),
        in_specs=[pl.BlockSpec(memory_space=pltpu.VMEM)],out_specs=pl.BlockSpec(memory_space=pltpu.VMEM),
        scratch_shapes=[pltpu.VMEM((n,n),jnp.float32),pltpu.VMEM((8,128),jnp.float32),pltpu.VMEM((128,128),jnp.float32)],
        compiler_params=pltpu.CompilerParams(vmem_limit_bytes=32*2**20),
        cost_estimate=pl.CostEstimate(flops=300_000_000*6,bytes_accessed=2**21,transcendentals=0))(g)


def body(contributions, valid_rows):
    blocks, height, width = contributions.shape
    live = jnp.arange(height, dtype=jnp.int32)[None, :] < valid_rows[:, None]
    frontal = jnp.where(live[:, :, None], contributions, 0.0).reshape(blocks * height, width)
    own = frontal[:, :LEAD]
    core = lax.axis_index("col")
    other = lax.ppermute(own, "col", [(0, 1), (1, 0)])
    lead = jnp.where(core == 0, own, other)
    gram = jnp.einsum("rp,rc->pc", lead, frontal, precision=HI)
    pieces = lax.all_to_all(gram.reshape(64, LEAD // 64, width), "row", 0, 0)
    mine = jnp.sum(pieces, axis=0)
    mine11 = mine[:, :LEAD]
    other11 = lax.ppermute(mine11, "col", [(0, 1), (1, 0)])
    mine11 = jnp.where(core == 0, mine11, other11)
    g11 = lax.all_to_all(jnp.broadcast_to(mine11[None], (64, LEAD // 64, LEAD)), "row", 0, 0)
    g11 = g11.reshape(LEAD, LEAD)
    mine, _ = lax.optimization_barrier((mine, g11[:8, :128]))
    gram_all = lax.all_gather(mine, "row", axis=0, tiled=True)
    inverse = inverse_factor(g11)
    projected = jnp.dot(inverse, gram_all, precision=HI)
    column_ids = core * width + jnp.arange(width, dtype=jnp.int32)
    kept = column_ids[None, :] >= jnp.arange(LEAD, dtype=jnp.int32)[:, None]
    return jnp.where(kept, projected, 0.0)


def solution(mesh):
    return jax.shard_map(
        body,
        mesh=mesh,
        in_specs=(P(("front", "row"), None, "col"), P(("front", "row"))),
        out_specs=P("front", "col"),
        check_vma=False,
    )
```

```python
import jax
import jax.numpy as jnp
from jax import lax
from jax.experimental import pallas as pl
from jax.experimental.pallas import tpu as pltpu
from jax.sharding import PartitionSpec as P

LEAD = 512
HI = lax.Precision.HIGHEST


S8=(8,128)
def lb(x,c): return jnp.broadcast_to(x[:,c:c+1],S8)
def sb(x,j): return jnp.broadcast_to(x[j:j+1,:],S8)

def chol_inv_128(V, sub, lane):
    V=list(V)
    E=[jnp.where(lane==sub+8*k,1.0,0.0) for k in range(16)]
    out=[]
    for k in range(16):
        X=V[k]
        LB=[lb(X,8*k+j) for j in range(8)]
        S=[[sb(LB[j],i) if i>=j else None for j in range(8)] for i in range(8)]
        R=[sb(X,j) for j in range(8)]
        F=[sb(E[k],j) for j in range(8)]
        l=[[None]*8 for _ in range(8)]
        inv=[None]*8
        for j in range(8):
            inv[j]=1.0/S[j][j]
            for i in range(j+1,8):
                l[i][j]=S[i][j]*inv[j]
                for m in range(j+1,i+1):
                    S[i][m]=S[i][m]-l[i][j]*S[m][j]
            for i in range(j+1,8):
                R[i]=R[i]-l[i][j]*R[j]
                F[i]=F[i]-l[i][j]*F[j]
        o=F[0]*lax.rsqrt(S[0][0])
        for j in range(1,8):
            o=jnp.where(sub==j,F[j]*lax.rsqrt(S[j][j]),o)
        out.append(o)
        if k<15:
            W=[R[j]*inv[j] for j in range(8)]
            H=[F[j]*inv[j] for j in range(8)]
            for i in range(7,0,-1):
                for j in range(i):
                    W[j]=W[j]-l[i][j]*W[i]
                    H[j]=H[j]-l[i][j]*H[i]
            for m in range(k+1,16):
                Y=V[m]; v=Y; e=E[m]
                for j in range(7,-1,-1):
                    c=lb(Y,8*k+j)
                    v=v-c*W[j]
                    e=e-c*H[j]
                V[m]=v; E[m]=e
    return out

def kernel(g_ref, o_ref, a, u, stack):
    a[...]=g_ref[...]
    o_ref[...]=jnp.zeros_like(o_ref)
    sub=lax.broadcasted_iota(jnp.int32,S8,0); lane=lax.broadcasted_iota(jnp.int32,S8,1)
    d=stack
    d[...]=g_ref[0:128,0:128]
    T=(((0,),(0,)),((),()))
    @pl.loop(0,4)
    def _(p):
        o=chol_inv_128([d[8*k:8*k+8,:] for k in range(16)],sub,lane)
        for k in range(16): d[8*k:8*k+8,:]=o[k]
        for q in range(4):
            @pl.when(p==q)
            def _():
                lo,hi=128*q,128*(q+1)
                linv=d[...]
                if q<3:
                    up=jnp.dot(linv,a[lo:hi,hi:],precision=HI,preferred_element_type=jnp.float32)
                    d[...]=a[hi:hi+128,hi:hi+128]-lax.dot_general(up[:,:128],up[:,:128],T,precision=HI,preferred_element_type=jnp.float32)
                    if q<2:
                        a[hi:,hi:]=a[hi:,hi:]-lax.dot_general(up,up,T,precision=HI,preferred_element_type=jnp.float32)
                o_ref[lo:hi,lo:hi]=linv
                if q>0:
                    o_ref[lo:hi,:lo]=jnp.dot(linv,o_ref[lo:hi,:lo],precision=HI,preferred_element_type=jnp.float32)
                if q<3:
                    o_ref[hi:,:hi]=o_ref[hi:,:hi]-lax.dot_general(up,o_ref[lo:hi,:hi],T,precision=HI,preferred_element_type=jnp.float32)

def inverse_factor(g):
    n=g.shape[0]
    return pl.pallas_call(kernel,out_shape=jax.ShapeDtypeStruct((n,n),jnp.float32),
        in_specs=[pl.BlockSpec(memory_space=pltpu.VMEM)],out_specs=pl.BlockSpec(memory_space=pltpu.VMEM),
        scratch_shapes=[pltpu.VMEM((n,n),jnp.float32),pltpu.VMEM((8,128),jnp.float32),pltpu.VMEM((128,128),jnp.float32)],
        compiler_params=pltpu.CompilerParams(vmem_limit_bytes=32*2**20),
        cost_estimate=pl.CostEstimate(flops=300_000_000*6,bytes_accessed=2**21,transcendentals=0))(g)


def flip(link):
    axis, kind = link
    pairs = []
    for chip in range(64):
        at = [chip % 4, chip // 4 % 4, chip // 16]
        for core in range(2):
            to = list(at)
            to[axis] ^= (1, 3)[kind ^ core]
            pairs.append((chip * 2 + core, (to[0] + 4 * to[1] + 16 * to[2]) * 2 + core))
    return pairs


XP, XM, YP, YM, ZP, ZM = [(axis, kind) for axis in range(3) for kind in range(2)]


def body(contributions, valid_rows):
    blocks, height, width = contributions.shape
    half = width // 2
    core = lax.axis_index("col")
    row = lax.axis_index("row")
    place = (row % 4, row // 4 % 4, row // 16)

    def bit(link):
        axis, kind = link
        high, low = place[axis] // 2, place[axis] % 2
        return jnp.where((core ^ kind) == 1, high, high ^ low) == 1

    def swap(x, link):
        return lax.ppermute(x, ("row", "col"), flip(link))

    def across(x):
        return lax.ppermute(x, "col", [(0, 1), (1, 0)])

    def halves(x, link):
        low, high = jnp.split(x, 2, axis=0)
        mine = bit(link)
        return jnp.where(mine, high, low), jnp.where(mine, low, high)

    def joined(own, got, link, axis):
        mine = bit(link)
        return jnp.concatenate([jnp.where(mine, got, own), jnp.where(mine, own, got)], axis=axis)

    def side(x, n):
        return jnp.concatenate(jnp.split(x, n, axis=0), axis=1)

    def stacked(x, n):
        return jnp.concatenate(jnp.split(x, n, axis=1), axis=0)

    live = jnp.arange(height, dtype=jnp.int32)[None, :] < valid_rows[:, None]
    frontal = jnp.where(live[:, :, None], contributions, 0.0).reshape(blocks * height, width)
    own = frontal[:, :LEAD]
    other = across(own)
    lead = jnp.where(core == 0, own, other)
    upper = bit(XP)
    kept = jnp.where(upper, frontal[:, half:], frontal[:, :half])
    given = jnp.where(upper, frontal[:, :half], frontal[:, half:])
    got = swap(jnp.concatenate([lead, given], axis=1), XP)
    lead = jnp.concatenate([lead, got[:, :LEAD]], axis=0)
    columns = jnp.concatenate([kept, got[:, LEAD:]], axis=0)
    quarter = 2 * core + upper.astype(jnp.int32)
    square = lax.dynamic_slice(lead, (0, quarter * 128), (lead.shape[0], 128))
    gram = jnp.einsum("rp,rc->pc", lead, jnp.concatenate([columns, square], axis=1), precision=HI)

    a, b, c, h = gram[:, :384], gram[:, 384:768], gram[:, 768:1024], gram[:, 1024:]
    a, a_out = halves(a, XM)
    b, b_out = halves(b, YP)
    ch, ch_out = halves(gram[:, 768:], ZP)
    ch = ch + swap(ch_out, ZP)
    a = a + swap(a_out, XM)
    b = b + swap(b_out, YP)
    c, h = ch[:, :256], ch[:, 256:]

    c, c_out = halves(c, XM)
    a, a_out = halves(a, YP)
    b, b_out = halves(b, ZP)
    ch = swap(jnp.concatenate([c_out, side(h, 2)], axis=1), XM)
    a = a + swap(a_out, YP)
    b = b + swap(b_out, ZP)
    c, h = c + ch[:, :256], h + stacked(ch[:, 256:], 2)

    c, c_out = halves(c, YP)
    a, a_out = halves(a, ZP)
    b, b_out = halves(b, XM)
    ch = swap(jnp.concatenate([c_out, side(h, 4)], axis=1), YP)
    a = a + swap(a_out, ZP)
    b = b + swap(b_out, XM)
    c, h = c + ch[:, :256], h + stacked(ch[:, 256:], 4)

    rest = jnp.concatenate([a, b, c], axis=1)
    for link in (YM, ZM):
        rest, out = halves(rest, link)
        n = out.shape[0]
        got = swap(jnp.concatenate([out, side(h, 8)], axis=0), link)
        rest, h = rest + got[:n], h + stacked(got[n:], 8)

    h = joined(h, swap(h, ZP), ZP, 0)
    h = joined(h, swap(h, XP), XP, 1)
    got = across(h)
    g11 = jnp.concatenate([jnp.where(core == 0, h, got), jnp.where(core == 0, got, h)], axis=1)
    inverse = inverse_factor(g11)

    rest = joined(rest, swap(rest, ZM), ZM, 0)
    rest = joined(rest, swap(rest, YM), YM, 0)
    got = swap(rest, XM)
    view = lambda x: x.reshape(1, 1, 1, 1, *x.shape)
    cut = lambda x: (view(x[:, :384]), view(x[:, 384:768]), view(x[:, 768:]))
    order = ((XM, YP, ZP), (YP, ZP, XM), (ZP, XM, YP))
    axis_of = lambda part, link: 0 if link == XP else 1 + order[part].index(link)
    parts = [joined(u, v, XM, axis_of(i, XM)) for i, (u, v) in enumerate(zip(cut(rest), cut(got)))]
    for step in ((YP, ZP, XP), (ZP, XP, YP), (XP, YP, ZP)):
        gots = [swap(parts[i], step[i]) for i in range(3)]
        parts = [joined(parts[i], gots[i], step[i], axis_of(i, step[i])) for i in range(3)]
    parts = [x.reshape(2, LEAD, x.shape[-1]) for x in parts]
    whole = jnp.concatenate([x[s] for s in range(2) for x in parts], axis=1)
    projected = jnp.dot(inverse, whole, precision=HI)
    column_ids = core * width + jnp.arange(width, dtype=jnp.int32)
    keep = column_ids[None, :] >= jnp.arange(LEAD, dtype=jnp.int32)[:, None]
    return jnp.where(keep, projected, 0.0)


def solution(mesh):
    return jax.shard_map(
        body,
        mesh=mesh,
        in_specs=(P(("front", "row"), None, "col"), P(("front", "row"))),
        out_specs=P("front", "col"),
        check_vma=False,
    )
```

```python
import jax
import jax.numpy as jnp
from jax import lax
from jax.experimental import pallas as pl
from jax.experimental.pallas import tpu as pltpu
from jax.sharding import PartitionSpec as P

LEAD = 512
HI = lax.Precision.HIGHEST


S8 = (8, 128)
F32 = jnp.float32
LEFT = (((0,), (0,)), ((), ()))


def lb(x, c):
    return jnp.broadcast_to(x[:, c : c + 1], S8)


def sb(x, j):
    return jnp.broadcast_to(x[j : j + 1, :], S8)


def mm(x, y):
    return jnp.dot(x, y, precision=HI, preferred_element_type=F32)


def mtm(x, y):
    return lax.dot_general(x, y, LEFT, precision=HI, preferred_element_type=F32)


def chol_inv_128(V, sub, lane):
    V=list(V)
    E=[jnp.where(lane==sub+8*k,1.0,0.0) for k in range(16)]
    out=[]
    for k in range(16):
        X=V[k]
        LB=[lb(X,8*k+j) for j in range(8)]
        S=[[sb(LB[j],i) if i>=j else None for j in range(8)] for i in range(8)]
        R=[sb(X,j) for j in range(8)]
        F=[sb(E[k],j) for j in range(8)]
        l=[[None]*8 for _ in range(8)]
        inv=[None]*8
        for j in range(8):
            inv[j]=1.0/S[j][j]
            for i in range(j+1,8):
                l[i][j]=S[i][j]*inv[j]
                for m in range(j+1,i+1):
                    S[i][m]=S[i][m]-l[i][j]*S[m][j]
            for i in range(j+1,8):
                R[i]=R[i]-l[i][j]*R[j]
                F[i]=F[i]-l[i][j]*F[j]
        o=F[0]*lax.rsqrt(S[0][0])
        for j in range(1,8):
            o=jnp.where(sub==j,F[j]*lax.rsqrt(S[j][j]),o)
        out.append(o)
        if k<15:
            W=[R[j]*inv[j] for j in range(8)]
            H=[F[j]*inv[j] for j in range(8)]
            for i in range(7,0,-1):
                for j in range(i):
                    W[j]=W[j]-l[i][j]*W[i]
                    H[j]=H[j]-l[i][j]*H[i]
            for m in range(k+1,16):
                Y=V[m]; v=Y; e=E[m]
                for j in range(7,-1,-1):
                    c=lb(Y,8*k+j)
                    v=v-c*W[j]
                    e=e-c*H[j]
                V[m]=v; E[m]=e
    return out


def vmem(*shape):
    return jax.ShapeDtypeStruct(shape, F32)


VMEM = pl.BlockSpec(memory_space=pltpu.VMEM)
PARAMS = pltpu.CompilerParams(vmem_limit_bytes=40 * 2**20)


def cost(flops, nbytes):
    return pl.CostEstimate(flops=flops, bytes_accessed=nbytes, transcendentals=0)


def factored(a_ref):
    sub = lax.broadcasted_iota(jnp.int32, S8, 0)
    lane = lax.broadcasted_iota(jnp.int32, S8, 1)
    return chol_inv_128([a_ref[8 * k : 8 * k + 8, 0:128] for k in range(16)], sub, lane)


def panel_kernel(a_ref, linv_ref, u_ref, next_ref):
    for k, block in enumerate(factored(a_ref)):
        linv_ref[8 * k : 8 * k + 8, :] = block
    u = mm(linv_ref[...], a_ref[:128, 128:])
    u_ref[...] = u
    next_ref[...] = a_ref[128:, 128:] - mtm(u, u)


def panel(a):
    n = a.shape[0] - 128
    return pl.pallas_call(
        panel_kernel,
        out_shape=(vmem(128, 128), vmem(128, n), vmem(n, n)),
        in_specs=[VMEM],
        out_specs=(VMEM, VMEM, VMEM),
        compiler_params=PARAMS,
        cost_estimate=cost(5_000_000_000, 1 << 20),
        name="panel",
    )(a)


def last_kernel(a_ref, l0, l1, l2, u0, u1, u2, o_ref):
    o_ref[...] = jnp.zeros_like(o_ref)
    o_ref[0:128, 0:128] = l0[...]
    o_ref[128:256, 128:256] = l1[...]
    o_ref[256:384, 256:384] = l2[...]
    o_ref[128:256, 0:128] = -mm(l1[...], mtm(u0[:, 0:128], l0[...]))
    t = mtm(u0[:, 128:256], o_ref[0:128, 0:256]) + mtm(u1[:, 0:128], o_ref[128:256, 0:256])
    o_ref[256:384, 0:256] = -mm(l2[...], t)
    t = mtm(u0[:, 256:384], o_ref[0:128, 0:384]) + mtm(u1[:, 128:256], o_ref[128:256, 0:384])
    t = t + mtm(u2[...], o_ref[256:384, 0:384])
    for k, block in enumerate(factored(a_ref)):
        o_ref[384 + 8 * k : 392 + 8 * k, 384:512] = block
    o_ref[384:512, 0:384] = -mm(o_ref[384:512, 384:512], t)


def last_panel(a, linvs, us):
    return pl.pallas_call(
        last_kernel,
        out_shape=vmem(512, 512),
        in_specs=[VMEM] * 7,
        out_specs=VMEM,
        compiler_params=PARAMS,
        cost_estimate=cost(6_000_000_000, 1 << 20),
        name="last_panel",
    )(a, *linvs, *us)


def two(x):
    high = x.astype(jnp.bfloat16)
    return high, (x - high.astype(F32)).astype(jnp.bfloat16)


def product_kernel(core_ref, inverse_ref, *refs):
    parts, out_ref, lh_ref, ll_ref, buf, sems = refs[:3], *refs[3:]
    lh_ref[...], ll_ref[...] = two(inverse_ref[...])
    width = out_ref.shape[1] // 2
    dot = lambda x, y: jnp.dot(x, y, preferred_element_type=F32)
    copies = []
    for s in range(2):
        at = s * width
        for part in parts:
            w = part.shape[-1]
            xh, xl = two(part[s])
            for r, n in ((0, 256), (256, 512)):
                lh, ll = lh_ref[r : r + 256, :n], ll_ref[r : r + 256, :n]
                y = dot(lh, xh[:n]) + (dot(lh, xl[:n]) + dot(ll, xh[:n]))
                if at < LEAD:
                    ids = core_ref[0] * 2 * width + at + lax.broadcasted_iota(jnp.int32, y.shape, 1)
                    y = jnp.where(ids >= r + lax.broadcasted_iota(jnp.int32, y.shape, 0), y, 0.0)
                buf[r : r + 256, at : at + w] = y
            place = (slice(None), pl.ds(at, w))
            copies.append(pltpu.make_async_copy(buf.at[place], out_ref.at[place], sems.at[len(copies)]))
            copies[-1].start()
            at += w
    for copy in copies:
        copy.wait()


def product(core, inverse, parts):
    return pl.pallas_call(
        product_kernel,
        out_shape=vmem(LEAD, 2048),
        in_specs=[pl.BlockSpec(memory_space=pltpu.SMEM)] + [VMEM] * 4,
        out_specs=pl.BlockSpec(memory_space=pl.ANY),
        scratch_shapes=[
            pltpu.VMEM((LEAD, LEAD), jnp.bfloat16),
            pltpu.VMEM((LEAD, LEAD), jnp.bfloat16),
            pltpu.VMEM((LEAD, 2048), F32),
            pltpu.SemaphoreType.DMA((6,)),
        ],
        compiler_params=PARAMS,
        cost_estimate=cost(3_000_000_000, 9 << 20),
        name="product",
    )(core.reshape(1), inverse, *parts)


def flip(link):
    axis, kind = link
    pairs = []
    for chip in range(64):
        at = [chip % 4, chip // 4 % 4, chip // 16]
        for core in range(2):
            to = list(at)
            to[axis] ^= (1, 3)[kind ^ core]
            pairs.append((chip * 2 + core, (to[0] + 4 * to[1] + 16 * to[2]) * 2 + core))
    return pairs


XP, XM, YP, YM, ZP, ZM = [(axis, kind) for axis in range(3) for kind in range(2)]


def body(contributions, valid_rows):
    blocks, height, width = contributions.shape
    half = width // 2
    core = lax.axis_index("col")
    row = lax.axis_index("row")
    place = (row % 4, row // 4 % 4, row // 16)

    def bit(link):
        axis, kind = link
        high, low = place[axis] // 2, place[axis] % 2
        return jnp.where((core ^ kind) == 1, high, high ^ low) == 1

    def swap(x, link):
        return lax.ppermute(x, ("row", "col"), flip(link))

    def across(x):
        return lax.ppermute(x, "col", [(0, 1), (1, 0)])

    def halves(x, link):
        low, high = jnp.split(x, 2, axis=0)
        mine = bit(link)
        return jnp.where(mine, high, low), jnp.where(mine, low, high)

    def joined(own, got, link, axis):
        mine = bit(link)
        return jnp.concatenate([jnp.where(mine, got, own), jnp.where(mine, own, got)], axis=axis)

    def side(x, n):
        return jnp.concatenate(jnp.split(x, n, axis=0), axis=1)

    def stacked(x, n):
        return jnp.concatenate(jnp.split(x, n, axis=1), axis=0)

    live = jnp.arange(height, dtype=jnp.int32)[None, :] < valid_rows[:, None]
    frontal = jnp.where(live[:, :, None], contributions, 0.0).reshape(blocks * height, width)
    own = frontal[:, :LEAD]
    other = across(own)
    lead = jnp.where(core == 0, own, other)
    upper = bit(XP)
    kept = jnp.where(upper, frontal[:, half:], frontal[:, :half])
    given = jnp.where(upper, frontal[:, :half], frontal[:, half:])
    got = swap(jnp.concatenate([lead, given], axis=1), XP)
    lead = jnp.concatenate([lead, got[:, :LEAD]], axis=0)
    columns = jnp.concatenate([kept, got[:, LEAD:]], axis=0)
    quarter = 2 * core + upper.astype(jnp.int32)
    square = lax.dynamic_slice(lead, (0, quarter * 128), (lead.shape[0], 128))
    gram = jnp.einsum("rp,rc->pc", lead, jnp.concatenate([columns, square], axis=1), precision=HI)

    a, b, c, h = gram[:, :384], gram[:, 384:768], gram[:, 768:1024], gram[:, 1024:]
    a, a_out = halves(a, XM)
    b, b_out = halves(b, YP)
    ch, ch_out = halves(gram[:, 768:], ZP)
    ch = ch + swap(ch_out, ZP)
    a = a + swap(a_out, XM)
    b = b + swap(b_out, YP)
    c, h = ch[:, :256], ch[:, 256:]

    c, c_out = halves(c, XM)
    a, a_out = halves(a, YP)
    b, b_out = halves(b, ZP)
    ch = swap(jnp.concatenate([c_out, side(h, 2)], axis=1), XM)
    a = a + swap(a_out, YP)
    b = b + swap(b_out, ZP)
    c, h = c + ch[:, :256], h + stacked(ch[:, 256:], 2)

    c, c_out = halves(c, YP)
    a, a_out = halves(a, ZP)
    b, b_out = halves(b, XM)
    ch = swap(jnp.concatenate([c_out, side(h, 4)], axis=1), YP)
    a = a + swap(a_out, ZP)
    b = b + swap(b_out, XM)
    c, h = c + ch[:, :256], h + stacked(ch[:, 256:], 4)

    rest = jnp.concatenate([a, b, c], axis=1)
    for link in (YM, ZM):
        rest, out = halves(rest, link)
        n = out.shape[0]
        got = swap(jnp.concatenate([out, side(h, 8)], axis=0), link)
        rest, h = rest + got[:n], h + stacked(got[n:], 8)

    h = joined(h, swap(h, ZP), ZP, 0)
    h = joined(h, swap(h, XP), XP, 1)
    got = across(h)
    g11 = jnp.concatenate([jnp.where(core == 0, h, got), jnp.where(core == 0, got, h)], axis=1)

    rest = joined(rest, swap(rest, ZM), ZM, 0)
    rest = joined(rest, swap(rest, YM), YM, 0)
    got = swap(rest, XM)
    view = lambda x: x.reshape(1, 1, 1, 1, *x.shape)
    cut = lambda x: (view(x[:, :384]), view(x[:, 384:768]), view(x[:, 768:]))
    order = ((XM, YP, ZP), (YP, ZP, XM), (ZP, XM, YP))
    axis_of = lambda part, link: 0 if link == XP else 1 + order[part].index(link)
    parts = [joined(u, v, XM, axis_of(i, XM)) for i, (u, v) in enumerate(zip(cut(rest), cut(got)))]
    linvs, us, a = [], [], g11
    for step in ((YP, ZP, XP), (ZP, XP, YP), (XP, YP, ZP)):
        gots = [swap(parts[i], step[i]) for i in range(3)]
        linv, u, a = panel(a)
        linvs.append(linv)
        us.append(u)
        parts = [joined(parts[i], gots[i], step[i], axis_of(i, step[i])) for i in range(3)]
    inverse = last_panel(a, linvs, us)
    return product(core, inverse, [x.reshape(2, LEAD, x.shape[-1]) for x in parts])


def solution(mesh):
    return jax.shard_map(
        body,
        mesh=mesh,
        in_specs=(P(("front", "row"), None, "col"), P(("front", "row"))),
        out_specs=P("front", "col"),
        check_vma=False,
    )
```

```python
import jax
import jax.numpy as jnp
from jax import lax
from jax.experimental import pallas as pl
from jax.experimental.pallas import tpu as pltpu
from jax.sharding import PartitionSpec as P

LEAD = 512
HI = lax.Precision.HIGHEST


S8 = (8, 128)
F32 = jnp.float32
LEFT = (((0,), (0,)), ((), ()))


def lb(x, c):
    return jnp.broadcast_to(x[:, c : c + 1], S8)


def sb(x, j):
    return jnp.broadcast_to(x[j : j + 1, :], S8)


def mm(x, y):
    return jnp.dot(x, y, precision=HI, preferred_element_type=F32)


def mtm(x, y):
    return lax.dot_general(x, y, LEFT, precision=HI, preferred_element_type=F32)


def chol_inv_128(V, sub, lane):
    V=list(V)
    E=[jnp.where(lane==sub+8*k,1.0,0.0) for k in range(16)]
    out=[]
    for k in range(16):
        X=V[k]
        LB=[lb(X,8*k+j) for j in range(8)]
        S=[[sb(LB[j],i) if i>=j else None for j in range(8)] for i in range(8)]
        R=[sb(X,j) for j in range(8)]
        F=[sb(E[k],j) for j in range(8)]
        l=[[None]*8 for _ in range(8)]
        inv=[None]*8
        for j in range(8):
            inv[j]=1.0/S[j][j]
            for i in range(j+1,8):
                l[i][j]=S[i][j]*inv[j]
                for m in range(j+1,i+1):
                    S[i][m]=S[i][m]-l[i][j]*S[m][j]
            for i in range(j+1,8):
                R[i]=R[i]-l[i][j]*R[j]
                F[i]=F[i]-l[i][j]*F[j]
        o=F[0]*lax.rsqrt(S[0][0])
        for j in range(1,8):
            o=jnp.where(sub==j,F[j]*lax.rsqrt(S[j][j]),o)
        out.append(o)
        if k<15:
            W=[R[j]*inv[j] for j in range(8)]
            H=[F[j]*inv[j] for j in range(8)]
            for i in range(7,0,-1):
                for j in range(i):
                    W[j]=W[j]-l[i][j]*W[i]
                    H[j]=H[j]-l[i][j]*H[i]
            for m in range(k+1,16):
                Y=V[m]; v=Y; e=E[m]
                for j in range(7,-1,-1):
                    c=lb(Y,8*k+j)
                    v=v-c*W[j]
                    e=e-c*H[j]
                V[m]=v; E[m]=e
    return out


def vmem(*shape):
    return jax.ShapeDtypeStruct(shape, F32)


VMEM = pl.BlockSpec(memory_space=pltpu.VMEM)
PARAMS = pltpu.CompilerParams(vmem_limit_bytes=40 * 2**20)


def cost(flops, nbytes):
    return pl.CostEstimate(flops=flops, bytes_accessed=nbytes, transcendentals=0)


def indexed(ref):
    return ref[0], ref[1], ref[2]


def aligned(i, n):
    return pl.ds(pl.multiple_of(i * n, n), n)


def call(kernel, out, index, args, flops=0, nbytes=1 << 20, scratch=(), out_specs=None, name=None):
    return pl.pallas_call(
        kernel,
        out_shape=out,
        in_specs=[pl.BlockSpec(memory_space=pltpu.SMEM)] + [VMEM] * len(args),
        out_specs=out_specs or jax.tree.map(lambda _: VMEM, out),
        scratch_shapes=list(scratch),
        compiler_params=PARAMS,
        cost_estimate=cost(flops, nbytes),
        name=name,
    )(index, *args)


def pack_kernel(index, x_ref, lead_ref, *outs):
    _, j, _ = indexed(index)
    for m, out in enumerate(outs):
        out[:, :LEAD] = lead_ref[...]
        out[:, LEAD:] = x_ref[:, aligned(j ^ m, 256)]


def gram_kernel(index, *refs):
    ins, outs, (lead, columns, gram) = refs[:8], refs[8:16], refs[16:]
    core, j, k = indexed(index)
    for m, ref in enumerate(ins):
        lead[128 * m : 128 * m + 128, :] = ref[:, :LEAD]
        columns[128 * m : 128 * m + 128, :] = ref[:, LEAD:]
    square = mtm(lead[:, aligned(j // 2, 128)], lead[:, aligned(core * 2 + j % 2, 128)])
    for out in outs:
        out[64:, :128] = square[:64]
        out[64:, 128:] = square[64:]
    gram[...] = mtm(lead[...], columns[...])
    for m, out in enumerate(outs):
        out[:64, :] = gram[aligned(k ^ m, 64), :]


def rows_kernel(index, *refs):
    _, _, k = indexed(index)
    for m in range(8):
        refs[8][aligned(k ^ m, 64), :] = refs[m][...]


def inverse_kernel(index, own, other, o_ref, a, d):
    core, j, k = indexed(index)
    for side, place, ref in ((core, j, own), (1 - core, k, other)):
        for m in range(8):
            at = place ^ m
            columns = aligned(side * 2 + at % 2, 128)
            a[aligned(at // 2 * 2, 64), columns] = ref[64 * m : 64 * m + 64, :128]
            a[aligned(at // 2 * 2 + 1, 64), columns] = ref[64 * m : 64 * m + 64, 128:]
    sub = lax.broadcasted_iota(jnp.int32, S8, 0)
    lane = lax.broadcasted_iota(jnp.int32, S8, 1)
    o_ref[...] = jnp.zeros_like(o_ref)
    d[...] = a[0:128, 0:128]

    @pl.loop(0, 4)
    def _(p):
        blocks = chol_inv_128([d[8 * i : 8 * i + 8, :] for i in range(16)], sub, lane)
        for i, block in enumerate(blocks):
            d[8 * i : 8 * i + 8, :] = block
        for q in range(4):

            @pl.when(p == q)
            def _():
                lo, hi = 128 * q, 128 * (q + 1)
                linv = d[...]
                if q < 3:
                    up = mm(linv, a[lo:hi, hi:])
                    d[...] = a[hi : hi + 128, hi : hi + 128] - mtm(up[:, :128], up[:, :128])
                    if q < 2:
                        a[hi:, hi:] = a[hi:, hi:] - mtm(up, up)
                o_ref[lo:hi, lo:hi] = linv
                if q > 0:
                    o_ref[lo:hi, :lo] = mm(linv, o_ref[lo:hi, :lo])
                if q < 3:
                    o_ref[hi:, :hi] = o_ref[hi:, :hi] - mtm(up, o_ref[lo:hi, :hi])


def two(x):
    high = x.astype(jnp.bfloat16)
    return high, (x - high.astype(F32)).astype(jnp.bfloat16)


def product_kernel(index, inverse_ref, *refs):
    parts, (out_ref, lh_ref, ll_ref, buf, sems) = refs[:8], refs[8:]
    core, j, _ = indexed(index)
    lh_ref[...], ll_ref[...] = two(inverse_ref[...])
    dot = lambda x, y: jnp.dot(x, y, preferred_element_type=F32)
    copies = []
    for m, part in enumerate(parts):
        xh, xl = two(part[...])
        for r, n in ((0, 256), (256, 512)):
            lh, ll = lh_ref[r : r + 256, :n], ll_ref[r : r + 256, :n]
            y = dot(lh, xh[:n]) + (dot(lh, xl[:n]) + dot(ll, xh[:n]))
            ids = core * 2048 + (j ^ m) * 256 + lax.broadcasted_iota(jnp.int32, y.shape, 1)
            y = jnp.where(ids >= r + lax.broadcasted_iota(jnp.int32, y.shape, 0), y, 0.0)
            buf[m, r : r + 256, :] = y
        copies.append(pltpu.make_async_copy(buf.at[m], out_ref.at[:, aligned(j ^ m, 256)], sems.at[m]))
        copies[-1].start()
    for copy in copies:
        copy.wait()


def flip(kind, mask):
    pairs = []
    for chip in range(64):
        for core in range(2):
            to = [chip % 4, chip // 4 % 4, chip // 16]
            for axis in range(3):
                if mask >> axis & 1:
                    to[axis] ^= (1, 3)[kind ^ core]
            pairs.append((chip * 2 + core, (to[0] + 4 * to[1] + 16 * to[2]) * 2 + core))
    return pairs


PLUS, MINUS = 0, 1


def exchange(kind, send):
    return [send(m) if m == 0 else lax.ppermute(send(m), ("row", "col"), flip(kind, m)) for m in range(8)]


def body(contributions, valid_rows):
    blocks, height, width = contributions.shape
    core = lax.axis_index("col")
    row = lax.axis_index("row")
    gray, high = 0, 0
    for axis, at in enumerate((row % 4, row // 4 % 4, row // 16)):
        high += at // 2 << axis
        gray += (at // 2 ^ at % 2) << axis
    index = jnp.stack([core, jnp.where(core == 0, gray, high), jnp.where(core == 0, high, gray)]).astype(jnp.int32)

    def across(x):
        return lax.ppermute(x, "col", [(0, 1), (1, 0)])

    live = jnp.arange(height, dtype=jnp.int32)[None, :] < valid_rows[:, None]
    frontal = jnp.where(live[:, :, None], contributions, 0.0).reshape(blocks * height, width)
    own = frontal[:, :LEAD]
    lead = jnp.where(core == 0, own, across(own))
    packed = call(pack_kernel, (vmem(128, 768),) * 8, index, (frontal, lead), name="pack")
    packed = exchange(PLUS, lambda m: packed[m])
    scratch = (pltpu.VMEM((1024, LEAD), F32), pltpu.VMEM((1024, 256), F32), pltpu.VMEM((LEAD, 256), F32))
    grams = call(gram_kernel, (vmem(128, 256),) * 8, index, packed, 1 << 30, 4 << 20, scratch, name="gram")
    g = exchange(MINUS, lambda m: grams[m])
    mine = ((g[0] + g[1]) + (g[2] + g[3])) + ((g[4] + g[5]) + (g[6] + g[7]))
    rest, square = mine[:64], mine[64:]
    square = jnp.concatenate(exchange(PLUS, lambda m: square), axis=0)
    rest = exchange(MINUS, lambda m: rest)
    rest = call(rows_kernel, vmem(LEAD, 256), index, rest, name="rows")
    scratch = (pltpu.VMEM((LEAD, LEAD), F32), pltpu.VMEM((128, 128), F32))
    inverse = call(inverse_kernel, vmem(LEAD, LEAD), index, (square, across(square)), 20 * 10**9, 2 << 20, scratch, name="inverse")
    parts = exchange(PLUS, lambda m: rest)
    scratch = (
        pltpu.VMEM((LEAD, LEAD), jnp.bfloat16),
        pltpu.VMEM((LEAD, LEAD), jnp.bfloat16),
        pltpu.VMEM((8, LEAD, 256), F32),
        pltpu.SemaphoreType.DMA((8,)),
    )
    spec = pl.BlockSpec(memory_space=pl.ANY)
    return call(product_kernel, vmem(LEAD, width), index, (inverse, *parts), 3 << 30, 9 << 20, scratch, spec, "product")


def solution(mesh):
    return jax.shard_map(
        body,
        mesh=mesh,
        in_specs=(P(("front", "row"), None, "col"), P(("front", "row"))),
        out_specs=P("front", "col"),
        check_vma=False,
    )
```

```python
import jax
import jax.numpy as jnp
from jax import lax
from jax.experimental import pallas as pl
from jax.experimental.pallas import tpu as pltpu
from jax.sharding import PartitionSpec as P

LEAD = 512
HI = lax.Precision.HIGHEST


S8 = (8, 128)
F32 = jnp.float32
LEFT = (((0,), (0,)), ((), ()))


def lb(x, c):
    return jnp.broadcast_to(x[:, c : c + 1], S8)


def sb(x, j):
    return jnp.broadcast_to(x[j : j + 1, :], S8)


def mm(x, y):
    return jnp.dot(x, y, precision=HI, preferred_element_type=F32)


def mtm(x, y):
    return lax.dot_general(x, y, LEFT, precision=HI, preferred_element_type=F32)


def chol_inv_128(V, sub, lane):
    V=list(V)
    E=[jnp.where(lane==sub+8*k,1.0,0.0) for k in range(16)]
    out=[]
    for k in range(16):
        X=V[k]
        LB=[lb(X,8*k+j) for j in range(8)]
        S=[[sb(LB[j],i) if i>=j else None for j in range(8)] for i in range(8)]
        R=[sb(X,j) for j in range(8)]
        F=[sb(E[k],j) for j in range(8)]
        l=[[None]*8 for _ in range(8)]
        inv=[None]*8
        for j in range(8):
            inv[j]=1.0/S[j][j]
            for i in range(j+1,8):
                l[i][j]=S[i][j]*inv[j]
                for m in range(j+1,i+1):
                    S[i][m]=S[i][m]-l[i][j]*S[m][j]
            for i in range(j+1,8):
                R[i]=R[i]-l[i][j]*R[j]
                F[i]=F[i]-l[i][j]*F[j]
        o=F[0]*lax.rsqrt(S[0][0])
        for j in range(1,8):
            o=jnp.where(sub==j,F[j]*lax.rsqrt(S[j][j]),o)
        out.append(o)
        if k<15:
            W=[R[j]*inv[j] for j in range(8)]
            H=[F[j]*inv[j] for j in range(8)]
            for i in range(7,0,-1):
                for j in range(i):
                    W[j]=W[j]-l[i][j]*W[i]
                    H[j]=H[j]-l[i][j]*H[i]
            for m in range(k+1,16):
                Y=V[m]; v=Y; e=E[m]
                for j in range(7,-1,-1):
                    c=lb(Y,8*k+j)
                    v=v-c*W[j]
                    e=e-c*H[j]
                V[m]=v; E[m]=e
    return out


def vmem(*shape):
    return jax.ShapeDtypeStruct(shape, F32)


VMEM = pl.BlockSpec(memory_space=pltpu.VMEM)
PARAMS = pltpu.CompilerParams(vmem_limit_bytes=40 * 2**20)


def cost(flops, nbytes):
    return pl.CostEstimate(flops=flops, bytes_accessed=nbytes, transcendentals=0)


def aligned(i, n):
    return pl.ds(pl.multiple_of(i * n, n), n)


def call(kernel, out, index, args, flops=0, nbytes=1 << 20, scratch=(), out_specs=None, name=None):
    return pl.pallas_call(
        kernel,
        out_shape=out,
        in_specs=[pl.BlockSpec(memory_space=pltpu.SMEM)] + [VMEM] * len(args),
        out_specs=out_specs or jax.tree.map(lambda _: VMEM, out),
        scratch_shapes=list(scratch),
        compiler_params=PARAMS,
        cost_estimate=cost(flops, nbytes),
        name=name,
    )(index, *args)


def pack_kernel(index, x_ref, lead_ref, out):
    for p in range(8):
        out[p, :, :LEAD] = lead_ref[...]
        out[p, :, LEAD:] = x_ref[:, 256 * p : 256 * p + 256]


def gram_kernel(index, x_ref, out):
    lead = x_ref[:, :LEAD]
    gram = mtm(lead, x_ref[:, LEAD:])
    square = mtm(lead, x_ref[:, aligned(index[0], 256)])
    for p in range(8):
        out[p, :64, :] = gram[64 * p : 64 * p + 64]
        out[p, 64:, :] = square[64 * p : 64 * p + 64]


def inverse_kernel(index, own, other, o_ref, a, d):
    a[:, aligned(index[0], 256)] = own[...]
    a[:, aligned(1 - index[0], 256)] = other[...]
    sub = lax.broadcasted_iota(jnp.int32, S8, 0)
    lane = lax.broadcasted_iota(jnp.int32, S8, 1)
    o_ref[...] = jnp.zeros_like(o_ref)
    d[...] = a[0:128, 0:128]

    @pl.loop(0, 4)
    def _(p):
        blocks = chol_inv_128([d[8 * i : 8 * i + 8, :] for i in range(16)], sub, lane)
        for i, block in enumerate(blocks):
            d[8 * i : 8 * i + 8, :] = block
        for q in range(4):

            @pl.when(p == q)
            def _():
                lo, hi = 128 * q, 128 * (q + 1)
                linv = d[...]
                if q < 3:
                    up = mm(linv, a[lo:hi, hi:])
                    d[...] = a[hi : hi + 128, hi : hi + 128] - mtm(up[:, :128], up[:, :128])
                    if q < 2:
                        a[hi:, hi:] = a[hi:, hi:] - mtm(up, up)
                o_ref[lo:hi, lo:hi] = linv
                if q > 0:
                    o_ref[lo:hi, :lo] = mm(linv, o_ref[lo:hi, :lo])
                if q < 3:
                    o_ref[hi:, :hi] = o_ref[hi:, :hi] - mtm(up, o_ref[lo:hi, :hi])


def two(x):
    high = x.astype(jnp.bfloat16)
    return high, (x - high.astype(F32)).astype(jnp.bfloat16)


def product_kernel(index, inverse_ref, parts, out_ref, lh_ref, ll_ref, buf, sems):
    lh_ref[...], ll_ref[...] = two(inverse_ref[...])
    dot = lambda x, y: jnp.dot(x, y, preferred_element_type=F32)
    copies = []
    for m in range(8):
        xh, xl = two(parts[m])
        for r, n in ((0, 256), (256, 512)):
            lh, ll = lh_ref[r : r + 256, :n], ll_ref[r : r + 256, :n]
            y = dot(lh, xh[:n]) + (dot(lh, xl[:n]) + dot(ll, xh[:n]))
            ids = index[0] * 2048 + m * 256 + lax.broadcasted_iota(jnp.int32, y.shape, 1)
            y = jnp.where(ids >= r + lax.broadcasted_iota(jnp.int32, y.shape, 0), y, 0.0)
            buf[m, r : r + 256, :] = y
        copies.append(pltpu.make_async_copy(buf.at[m], out_ref.at[:, pl.ds(256 * m, 256)], sems.at[m]))
        copies[-1].start()
    for copy in copies:
        copy.wait()


def cubes(kind):
    groups = {}
    for chip in range(64):
        at = (chip % 4, chip // 4 % 4, chip // 16)
        high = sum(a // 2 << i for i, a in enumerate(at))
        gray = sum((a // 2 ^ a % 2) << i for i, a in enumerate(at))
        for core in range(2):
            inside, outside = (gray, high) if core == kind else (high, gray)
            groups.setdefault((core, outside), {})[inside] = chip * 2 + core
    return [[group[i] for i in range(8)] for _, group in sorted(groups.items())]


PLUS, MINUS = cubes(0), cubes(1)


def exchange(x, groups):
    return lax.all_to_all(x, ("row", "col"), 0, 0, axis_index_groups=groups)


def body(contributions, valid_rows):
    blocks, height, width = contributions.shape
    core = lax.axis_index("col")
    index = core.reshape(1)

    def across(x):
        return lax.ppermute(x, "col", [(0, 1), (1, 0)])

    def copies(x):
        return jnp.broadcast_to(x[None], (8, *x.shape))

    live = jnp.arange(height, dtype=jnp.int32)[None, :] < valid_rows[:, None]
    frontal = jnp.where(live[:, :, None], contributions, 0.0).reshape(blocks * height, width)
    own = frontal[:, :LEAD]
    lead = jnp.where(core == 0, own, across(own))
    packed = exchange(call(pack_kernel, vmem(8, 128, 768), index, (frontal, lead), name="pack"), PLUS)
    grams = call(gram_kernel, vmem(8, 128, 256), index, (packed.reshape(1024, 768),), 1 << 30, 4 << 20, name="gram")
    mine = jnp.sum(exchange(grams, MINUS), axis=0)
    whole = exchange(copies(mine), MINUS)
    rest, square = whole[:, :64].reshape(LEAD, 256), whole[:, 64:].reshape(LEAD, 256)
    parts = exchange(copies(rest), PLUS)
    scratch = (pltpu.VMEM((LEAD, LEAD), F32), pltpu.VMEM((128, 128), F32))
    inverse = call(inverse_kernel, vmem(LEAD, LEAD), index, (square, across(square)), 20 * 10**9, 2 << 20, scratch, name="inverse")
    scratch = (
        pltpu.VMEM((LEAD, LEAD), jnp.bfloat16),
        pltpu.VMEM((LEAD, LEAD), jnp.bfloat16),
        pltpu.VMEM((8, LEAD, 256), F32),
        pltpu.SemaphoreType.DMA((8,)),
    )
    spec = pl.BlockSpec(memory_space=pl.ANY)
    return call(product_kernel, vmem(LEAD, width), index, (inverse, parts), 3 << 30, 9 << 20, scratch, spec, "product")


def solution(mesh):
    return jax.shard_map(
        body,
        mesh=mesh,
        in_specs=(P(("front", "row"), None, "col"), P(("front", "row"))),
        out_specs=P("front", "col"),
        check_vma=False,
    )
```

```python
import jax
import jax.numpy as jnp
from jax import lax
from jax.experimental import pallas as pl
from jax.experimental.pallas import tpu as pltpu
from jax.sharding import PartitionSpec as P

LEAD = 512
HI = lax.Precision.HIGHEST


S8 = (8, 128)
F32 = jnp.float32
LEFT = (((0,), (0,)), ((), ()))


def lb(x, c):
    return jnp.broadcast_to(x[:, c : c + 1], S8)


def sb(x, j):
    return jnp.broadcast_to(x[j : j + 1, :], S8)


def mm(x, y):
    return jnp.dot(x, y, precision=HI, preferred_element_type=F32)


def mtm(x, y):
    return lax.dot_general(x, y, LEFT, precision=HI, preferred_element_type=F32)


def chol_inv_128(V, sub, lane):
    V=list(V)
    E=[jnp.where(lane==sub+8*k,1.0,0.0) for k in range(16)]
    out=[]
    for k in range(16):
        X=V[k]
        LB=[lb(X,8*k+j) for j in range(8)]
        S=[[sb(LB[j],i) if i>=j else None for j in range(8)] for i in range(8)]
        R=[sb(X,j) for j in range(8)]
        F=[sb(E[k],j) for j in range(8)]
        l=[[None]*8 for _ in range(8)]
        inv=[None]*8
        if k<15:
            Y1=V[k+1]
            C=[lb(Y1,8*k+j) for j in range(8)]
            v1=Y1; e1=E[k+1]
        for j in range(8):
            if j<7: sq=S[j+1][j]*S[j+1][j]
            inv[j]=1.0/S[j][j]
            if j<7: S[j+1][j+1]=S[j+1][j+1]-sq*inv[j]
            for i in range(j+1,8):
                l[i][j]=S[i][j]*inv[j]
                for m in range(j+1,i+1):
                    if not (i==j+1 and m==j+1):
                        S[i][m]=S[i][m]-l[i][j]*S[m][j]
            if k<15:
                c=C[j]*inv[j]
                v1=v1-c*R[j]
                e1=e1-c*F[j]
                for i in range(j+1,8):
                    C[i]=C[i]-l[i][j]*C[j]
            for i in range(j+1,8):
                R[i]=R[i]-l[i][j]*R[j]
                F[i]=F[i]-l[i][j]*F[j]
        o=F[0]*lax.rsqrt(S[0][0])
        for j in range(1,8):
            o=jnp.where(sub==j,F[j]*lax.rsqrt(S[j][j]),o)
        out.append(o)
        if k<15:
            V[k+1]=v1; E[k+1]=e1
        if k<14:
            W=[R[j]*inv[j] for j in range(8)]
            H=[F[j]*inv[j] for j in range(8)]
            for i in range(7,0,-1):
                for j in range(i):
                    W[j]=W[j]-l[i][j]*W[i]
                    H[j]=H[j]-l[i][j]*H[i]
            for m in range(k+2,16):
                Y=V[m]; v=Y; e=E[m]
                for j in range(7,-1,-1):
                    c=lb(Y,8*k+j)
                    v=v-c*W[j]
                    e=e-c*H[j]
                V[m]=v; E[m]=e
    return out


def vmem(*shape):
    return jax.ShapeDtypeStruct(shape, F32)


VMEM = pl.BlockSpec(memory_space=pltpu.VMEM)


def cost(flops, nbytes):
    return pl.CostEstimate(flops=flops, bytes_accessed=nbytes, transcendentals=0)


def aligned(i, n):
    return pl.ds(pl.multiple_of(i * n, n), n)


def call(kernel, out, index, args, flops=0, nbytes=1 << 20, scratch=(), out_specs=None, name=None, limit=12):
    return pl.pallas_call(
        kernel,
        out_shape=out,
        in_specs=[pl.BlockSpec(memory_space=pltpu.SMEM)] + [VMEM] * len(args),
        out_specs=out_specs or jax.tree.map(lambda _: VMEM, out),
        scratch_shapes=list(scratch),
        compiler_params=pltpu.CompilerParams(vmem_limit_bytes=limit << 20),
        cost_estimate=cost(flops, nbytes),
        name=name,
    )(index, *args)


def pack_kernel(index, x_ref, other_ref, out):
    live = lax.broadcasted_iota(jnp.int32, (128, LEAD), 0) < index[1]
    lead = jnp.where(live, jnp.where(index[0] == 0, x_ref[:, :LEAD], other_ref[...]), 0.0)
    for p in range(8):
        out[p, :, :LEAD] = lead
        out[p, :, LEAD:] = jnp.where(live[:, :256], x_ref[:, 256 * p : 256 * p + 256], 0.0)


def gram_kernel(index, x_ref, out):
    lead = x_ref[:, :LEAD]
    gram = mtm(lead, x_ref[:, LEAD:])
    square = mtm(lead, x_ref[:, aligned(index[0], 256)])
    for p in range(8):
        out[p, :64, :] = gram[64 * p : 64 * p + 64]
        out[p, 64:, :] = square[64 * p : 64 * p + 64]


def inverse_kernel(index, own, other, o_ref, a, d):
    a[:, aligned(index[0], 256)] = own[...]
    a[:, aligned(1 - index[0], 256)] = other[...]
    sub = lax.broadcasted_iota(jnp.int32, S8, 0)
    lane = lax.broadcasted_iota(jnp.int32, S8, 1)
    o_ref[...] = jnp.zeros_like(o_ref)
    d[...] = a[0:128, 0:128]

    @pl.loop(0, 4)
    def _(p):
        blocks = chol_inv_128([d[8 * i : 8 * i + 8, :] for i in range(16)], sub, lane)
        for i, block in enumerate(blocks):
            d[8 * i : 8 * i + 8, :] = block
        for q in range(4):

            @pl.when(p == q)
            def _():
                lo, hi = 128 * q, 128 * (q + 1)
                linv = d[...]
                if q < 3:
                    up = mm(linv, a[lo:hi, hi:])
                    d[...] = a[hi : hi + 128, hi : hi + 128] - mtm(up[:, :128], up[:, :128])
                    if q < 2:
                        a[hi:, hi:] = a[hi:, hi:] - mtm(up, up)
                o_ref[lo:hi, lo:hi] = linv
                if q > 0:
                    o_ref[lo:hi, :lo] = mm(linv, o_ref[lo:hi, :lo])
                if q < 3:
                    o_ref[hi:, :hi] = o_ref[hi:, :hi] - mtm(up, o_ref[lo:hi, :hi])


def two(x):
    high = x.astype(jnp.bfloat16)
    return high, (x - high.astype(F32)).astype(jnp.bfloat16)


def product_kernel(index, inverse_ref, parts, out_ref, lh_ref, ll_ref, buf, sems):
    lh_ref[...], ll_ref[...] = two(inverse_ref[...])
    dot = lambda x, y: jnp.dot(x, y, preferred_element_type=F32)
    copies = []
    for m in range(8):
        xh, xl = two(parts[m])
        for r, n in ((0, 256), (256, 512)):
            lh, ll = lh_ref[r : r + 256, :n], ll_ref[r : r + 256, :n]
            y = dot(lh, xh[:n]) + (dot(lh, xl[:n]) + dot(ll, xh[:n]))
            ids = index[0] * 2048 + m * 256 + lax.broadcasted_iota(jnp.int32, y.shape, 1)
            y = jnp.where(ids >= r + lax.broadcasted_iota(jnp.int32, y.shape, 0), y, 0.0)
            buf[m, r : r + 256, :] = y
        copies.append(pltpu.make_async_copy(buf.at[m], out_ref.at[:, pl.ds(256 * m, 256)], sems.at[m]))
        copies[-1].start()
    for copy in copies:
        copy.wait()


def cubes(kind):
    groups = {}
    for chip in range(64):
        for core in range(2):
            inside = outside = 0
            for axis, at in enumerate((chip % 4, chip // 4 % 4, chip // 16)):
                bits = (at // 2 ^ at % 2, at // 2)
                first = kind ^ core ^ (axis == 1)
                inside += bits[first] << axis
                outside += bits[1 - first] << axis
            groups.setdefault((core, outside), {})[inside] = chip * 2 + core
    return [[group[i] for i in range(8)] for _, group in sorted(groups.items())]


PLUS, MINUS = cubes(0), cubes(1)


def exchange(x, groups):
    return lax.all_to_all(x, ("row", "col"), 0, 0, axis_index_groups=groups)


def body(contributions, valid_rows):
    blocks, height, width = contributions.shape
    core = lax.axis_index("col")
    index = core.reshape(1)

    def across(x):
        return lax.ppermute(x, "col", [(0, 1), (1, 0)])

    def copies(x):
        return jnp.broadcast_to(x[None], (8, *x.shape))

    raw = contributions.reshape(blocks * height, width)
    limits = jnp.stack([core, valid_rows[0]])
    packed = call(pack_kernel, vmem(8, 128, 768), limits, (raw, across(raw[:, :LEAD])), name="pack")
    packed = exchange(packed, PLUS)
    grams = call(gram_kernel, vmem(8, 128, 256), index, (packed.reshape(1024, 768),), 1 << 30, 4 << 20, name="gram", limit=24)
    mine = jnp.sum(exchange(grams, MINUS), axis=0)
    whole = exchange(copies(mine), MINUS)
    rest, square = whole[:, :64].reshape(LEAD, 256), whole[:, 64:].reshape(LEAD, 256)
    parts = exchange(copies(rest), PLUS)
    scratch = (pltpu.VMEM((LEAD, LEAD), F32), pltpu.VMEM((128, 128), F32))
    inverse = call(inverse_kernel, vmem(LEAD, LEAD), index, (square, across(square)), 20 * 10**9, 2 << 20, scratch, name="inverse")
    scratch = (
        pltpu.VMEM((LEAD, LEAD), jnp.bfloat16),
        pltpu.VMEM((LEAD, LEAD), jnp.bfloat16),
        pltpu.VMEM((8, LEAD, 256), F32),
        pltpu.SemaphoreType.DMA((8,)),
    )
    spec = pl.BlockSpec(memory_space=pl.ANY)
    return call(product_kernel, vmem(LEAD, width), index, (inverse, parts), 3 << 30, 9 << 20, scratch, spec, "product", 24)


def solution(mesh):
    return jax.shard_map(
        body,
        mesh=mesh,
        in_specs=(P(("front", "row"), None, "col"), P(("front", "row"))),
        out_specs=P("front", "col"),
        check_vma=False,
    )
```

```python
import jax
import jax.numpy as jnp
from jax import lax
from jax.experimental import pallas as pl
from jax.experimental.pallas import tpu as pltpu
from jax.sharding import PartitionSpec as P

LEAD = 512
HI = lax.Precision.HIGHEST


S8 = (8, 128)
F32 = jnp.float32
LEFT = (((0,), (0,)), ((), ()))


def lb(x, c):
    return jnp.broadcast_to(x[:, c : c + 1], S8)


def sb(x, j):
    return jnp.broadcast_to(x[j : j + 1, :], S8)


def mm(x, y):
    return jnp.dot(x, y, precision=HI, preferred_element_type=F32)


def mtm(x, y):
    return lax.dot_general(x, y, LEFT, precision=HI, preferred_element_type=F32)


def chol_inv_128(V, sub, lane):
    V=list(V)
    E=[jnp.where(lane==sub+8*k,1.0,0.0) for k in range(16)]
    out=[]
    for k in range(16):
        X=V[k]
        LB=[lb(X,8*k+j) for j in range(8)]
        S=[[sb(LB[j],i) if i>=j else None for j in range(8)] for i in range(8)]
        R=[sb(X,j) for j in range(8)]
        F=[sb(E[k],j) for j in range(8)]
        l=[[None]*8 for _ in range(8)]
        inv=[None]*8
        if k<15:
            Y1=V[k+1]
            C=[lb(Y1,8*k+j) for j in range(8)]
            v1=Y1; e1=E[k+1]
        for j in range(8):
            if j<7: sq=S[j+1][j]*S[j+1][j]
            inv[j]=1.0/S[j][j]
            if j<7: S[j+1][j+1]=S[j+1][j+1]-sq*inv[j]
            for i in range(j+1,8):
                l[i][j]=S[i][j]*inv[j]
                for m in range(j+1,i+1):
                    if not (i==j+1 and m==j+1):
                        S[i][m]=S[i][m]-l[i][j]*S[m][j]
            if k<15:
                c=C[j]*inv[j]
                v1=v1-c*R[j]
                e1=e1-c*F[j]
                for i in range(j+1,8):
                    C[i]=C[i]-l[i][j]*C[j]
            for i in range(j+1,8):
                R[i]=R[i]-l[i][j]*R[j]
                F[i]=F[i]-l[i][j]*F[j]
        o=F[0]*lax.rsqrt(S[0][0])
        for j in range(1,8):
            o=jnp.where(sub==j,F[j]*lax.rsqrt(S[j][j]),o)
        out.append(o)
        if k<15:
            V[k+1]=v1; E[k+1]=e1
        if k<14:
            W=[R[j]*inv[j] for j in range(8)]
            H=[F[j]*inv[j] for j in range(8)]
            for i in range(7,0,-1):
                for j in range(i):
                    W[j]=W[j]-l[i][j]*W[i]
                    H[j]=H[j]-l[i][j]*H[i]
            for m in range(k+2,16):
                Y=V[m]; v=Y; e=E[m]
                for j in range(7,-1,-1):
                    c=lb(Y,8*k+j)
                    v=v-c*W[j]
                    e=e-c*H[j]
                V[m]=v; E[m]=e
    return out


def vmem(*shape):
    return jax.ShapeDtypeStruct(shape, F32)


VMEM = pl.BlockSpec(memory_space=pltpu.VMEM)


def cost(flops, nbytes):
    return pl.CostEstimate(flops=flops, bytes_accessed=nbytes, transcendentals=0)


def aligned(i, n):
    return pl.ds(pl.multiple_of(i * n, n), n)


def call(kernel, out, index, args, flops=0, nbytes=1 << 20, scratch=(), out_specs=None, name=None, limit=12):
    return pl.pallas_call(
        kernel,
        out_shape=out,
        in_specs=[pl.BlockSpec(memory_space=pltpu.SMEM)] + [VMEM] * len(args),
        out_specs=out_specs or jax.tree.map(lambda _: VMEM, out),
        scratch_shapes=list(scratch),
        compiler_params=pltpu.CompilerParams(vmem_limit_bytes=limit << 20),
        cost_estimate=cost(flops, nbytes),
        name=name,
    )(index, *args)


def pack_kernel(index, x_ref, other_ref, out):
    live = lax.broadcasted_iota(jnp.int32, (128, LEAD), 0) < index[1]
    lead = jnp.where(live, jnp.where(index[0] == 0, x_ref[:, :LEAD], other_ref[...]), 0.0)
    for p in range(8):
        out[p, :, :LEAD] = lead
        out[p, :, LEAD:] = jnp.where(live[:, :256], x_ref[:, 256 * p : 256 * p + 256], 0.0)


def gram_kernel(index, x_ref, out):
    lead = x_ref[:, :LEAD]
    gram = mtm(lead, x_ref[:, LEAD:])
    square = mtm(lead, x_ref[:, aligned(index[0], 256)])
    for p in range(8):
        out[p, :64, :] = gram[64 * p : 64 * p + 64]
        out[p, 64:, :] = square[64 * p : 64 * p + 64]


def panels(first, d, a, o_ref):
    sub = lax.broadcasted_iota(jnp.int32, S8, 0)
    lane = lax.broadcasted_iota(jnp.int32, S8, 1)
    base = 128 * first
    d[...] = a[0:128, 0:128]

    @pl.loop(0, 2)
    def _(p):
        blocks = chol_inv_128([d[8 * i : 8 * i + 8, :] for i in range(16)], sub, lane)
        for i, block in enumerate(blocks):
            d[8 * i : 8 * i + 8, :] = block
        for q in range(2):

            @pl.when(p == q)
            def _():
                lo, hi = 128 * q, 128 * (q + 1)
                glo, ghi = base + lo, base + hi
                linv = d[...]
                if ghi < LEAD:
                    up = mm(linv, a[lo:hi, hi:])
                    left = a[hi:, hi:] - mtm(up, up)
                    a[hi:, hi:] = left
                    d[...] = left[:128, :128]
                o_ref[glo:ghi, glo:ghi] = linv
                if glo > 0:
                    o_ref[glo:ghi, :glo] = mm(linv, o_ref[glo:ghi, :glo])
                if ghi < LEAD:
                    o_ref[ghi:, :ghi] = o_ref[ghi:, :ghi] - mtm(up, o_ref[glo:ghi, :ghi])


def first_kernel(index, own, other, o_ref, left_ref, token, a, d):
    a[:, aligned(index[0], 256)] = own[...]
    a[:, aligned(1 - index[0], 256)] = other[...]
    o_ref[...] = jnp.zeros_like(o_ref)
    panels(0, d, a, o_ref)
    left_ref[...] = a[256:, 256:]
    token[0] = jnp.int32(0)


def second_kernel(index, half_ref, left_ref, o_ref, a, d):
    o_ref[...] = half_ref[...]
    a[...] = left_ref[...]
    panels(2, d, a, o_ref)


def two(x):
    high = x.astype(jnp.bfloat16)
    return high, (x - high.astype(F32)).astype(jnp.bfloat16)


def product_kernel(index, inverse_ref, *refs):
    parts, (out_ref, lh_ref, ll_ref, buf, sems) = refs[:8], refs[8:]
    lh_ref[...], ll_ref[...] = two(inverse_ref[...])
    dot = lambda x, y: jnp.dot(x, y, preferred_element_type=F32)
    copies = []
    for m in range(8):
        xh, xl = two(parts[m][...])
        for r, n in ((0, 256), (256, 512)):
            lh, ll = lh_ref[r : r + 256, :n], ll_ref[r : r + 256, :n]
            y = dot(lh, xh[:n]) + (dot(lh, xl[:n]) + dot(ll, xh[:n]))
            ids = index[0] * 2048 + (index[1] ^ m) * 256 + lax.broadcasted_iota(jnp.int32, y.shape, 1)
            y = jnp.where(ids >= r + lax.broadcasted_iota(jnp.int32, y.shape, 0), y, 0.0)
            buf[m, r : r + 256, :] = y
        copies.append(pltpu.make_async_copy(buf.at[m], out_ref.at[:, aligned(index[1] ^ m, 256)], sems.at[m]))
        copies[-1].start()
    for copy in copies:
        copy.wait()


def cubes(kind):
    groups = {}
    for chip in range(64):
        for core in range(2):
            inside = outside = 0
            for axis, at in enumerate((chip % 4, chip // 4 % 4, chip // 16)):
                bits = (at // 2 ^ at % 2, at // 2)
                first = kind ^ core ^ (axis == 1)
                inside += bits[first] << axis
                outside += bits[1 - first] << axis
            groups.setdefault((core, outside), {})[inside] = chip * 2 + core
    return [[group[i] for i in range(8)] for _, group in sorted(groups.items())]


PLUS, MINUS = cubes(0), cubes(1)


def flip(mask):
    return [(group[i], group[i ^ mask]) for group in PLUS for i in range(8)]


def exchange(x, groups):
    return lax.all_to_all(x, ("row", "col"), 0, 0, axis_index_groups=groups)


def body(contributions, valid_rows):
    blocks, height, width = contributions.shape
    core = lax.axis_index("col")
    row = lax.axis_index("row")
    index = core.reshape(1)

    def across(x):
        return lax.ppermute(x, "col", [(0, 1), (1, 0)])

    def copies(x):
        return jnp.broadcast_to(x[None], (8, *x.shape))

    raw = contributions.reshape(blocks * height, width)
    limits = jnp.stack([core, valid_rows[0]])
    packed = call(pack_kernel, vmem(8, 128, 768), limits, (raw, across(raw[:, :LEAD])), name="pack")
    packed = exchange(packed, PLUS)
    grams = call(gram_kernel, vmem(8, 128, 256), index, (packed.reshape(1024, 768),), 1 << 30, 4 << 20, name="gram", limit=24)
    mine = jnp.sum(exchange(grams, MINUS), axis=0)
    whole = exchange(copies(mine), MINUS)
    rest, square = whole[:, :64].reshape(LEAD, 256), whole[:, 64:].reshape(LEAD, 256)
    def swap(x, mask):
        return lax.ppermute(x, ("row", "col"), flip(mask))

    near = [swap(rest, mask) for mask in (1, 2, 4)]
    far = swap(rest, 7)
    out = (vmem(LEAD, LEAD), vmem(256, 256), jax.ShapeDtypeStruct((1,), jnp.int32))
    scratch = (pltpu.VMEM((LEAD, LEAD), F32), pltpu.VMEM((128, 128), F32))
    specs = (VMEM, VMEM, pl.BlockSpec(memory_space=pltpu.SMEM))
    half, left, token = call(first_kernel, out, index, (square, across(square)), 10**10, 2 << 20, scratch, specs, "first")
    scratch = (pltpu.VMEM((256, 256), F32), pltpu.VMEM((128, 128), F32))
    inverse = call(second_kernel, vmem(LEAD, LEAD), index, (half, left), 10**10, 2 << 20, scratch, name="second")
    zero = token[0].astype(F32)
    x, y, z = (block + zero for block in near)
    xy, yz, zx = swap(y, 1), swap(z, 2), swap(x, 4)
    parts = (rest, near[0], near[1], xy, near[2], zx, yz, far)
    place = 0
    for axis, at in enumerate((row % 4, row // 4 % 4, row // 16)):
        high, gray = at // 2, at // 2 ^ at % 2
        place += jnp.where((core ^ int(axis == 1)) == 0, gray, high) << axis
    index = jnp.stack([core, place]).astype(jnp.int32)
    scratch = (
        pltpu.VMEM((LEAD, LEAD), jnp.bfloat16),
        pltpu.VMEM((LEAD, LEAD), jnp.bfloat16),
        pltpu.VMEM((8, LEAD, 256), F32),
        pltpu.SemaphoreType.DMA((8,)),
    )
    spec = pl.BlockSpec(memory_space=pl.ANY)
    return call(product_kernel, vmem(LEAD, width), index, (inverse, *parts), 3 << 30, 9 << 20, scratch, spec, "product", 24)


def solution(mesh):
    return jax.shard_map(
        body,
        mesh=mesh,
        in_specs=(P(("front", "row"), None, "col"), P(("front", "row"))),
        out_specs=P("front", "col"),
        check_vma=False,
    )
```

```python
import jax
import jax.numpy as jnp
from jax import lax
from jax.experimental import pallas as pl
from jax.experimental.pallas import tpu as pltpu
from jax.sharding import PartitionSpec as P

LEAD = 512
HI = lax.Precision.HIGHEST


S8 = (8, 128)
F32 = jnp.float32
LEFT = (((0,), (0,)), ((), ()))


def lb(x, c):
    return jnp.broadcast_to(x[:, c : c + 1], S8)


def sb(x, j):
    return jnp.broadcast_to(x[j : j + 1, :], S8)


def mm(x, y):
    return jnp.dot(x, y, precision=HI, preferred_element_type=F32)


def mtm(x, y):
    return lax.dot_general(x, y, LEFT, precision=HI, preferred_element_type=F32)


def chol_inv_128(V, sub, lane):
    V=list(V)
    E=[jnp.where(lane==sub+8*k,1.0,0.0) for k in range(16)]
    out=[]
    for k in range(16):
        X=V[k]
        LB=[lb(X,8*k+j) for j in range(8)]
        S=[[sb(LB[j],i) if i>=j else None for j in range(8)] for i in range(8)]
        R=[sb(X,j) for j in range(8)]
        F=[sb(E[k],j) for j in range(8)]
        l=[[None]*8 for _ in range(8)]
        inv=[None]*8
        if k<15:
            Y1=V[k+1]
            C=[lb(Y1,8*k+j) for j in range(8)]
            v1=Y1; e1=E[k+1]
        for j in range(0,8,2):
            a,b,c=S[j][j],S[j+1][j],S[j+1][j+1]
            det=a*c-b*b
            both=1.0/det
            inv[j]=1.0/a
            inv[j+1]=a*both
            l[j+1][j]=b*inv[j]
            S[j+1][j+1]=det*inv[j]
            p={i:S[i][j] for i in range(j+2,8)}
            q={i:S[i][j+1] for i in range(j+2,8)}
            r={}
            near={}
            for i in range(j+2,min(j+4,8)):
                for m in range(j+2,i+1):
                    n=(c*p[i])*p[m]-b*(p[i]*q[m]+q[i]*p[m])+(a*q[i])*q[m] if i!=m else (c*p[i])*p[i]-(b+b)*(p[i]*q[i])+(a*q[i])*q[i]
                    near[i,m]=S[i][m]-n*both
            for i in range(j+2,8):
                l[i][j]=p[i]*inv[j]
                r[i]=q[i]-l[i][j]*b
                l[i][j+1]=r[i]*inv[j+1]
                for m in range(j+2,i+1):
                    S[i][m]=near[i,m] if (i,m) in near else S[i][m]-l[i][j]*p[m]-l[i][j+1]*r[m]
            for t in (j,j+1):
                if k<15:
                    cc=C[t]*inv[t]
                    v1=v1-cc*R[t]
                    e1=e1-cc*F[t]
                    for i in range(t+1,8):
                        C[i]=C[i]-l[i][t]*C[t]
                for i in range(t+1,8):
                    R[i]=R[i]-l[i][t]*R[t]
                    F[i]=F[i]-l[i][t]*F[t]
        o=F[0]*lax.rsqrt(S[0][0])
        for j in range(1,8):
            o=jnp.where(sub==j,F[j]*lax.rsqrt(S[j][j]),o)
        out.append(o)
        if k<15:
            V[k+1]=v1; E[k+1]=e1
        if k<14:
            W=[R[j]*inv[j] for j in range(8)]
            H=[F[j]*inv[j] for j in range(8)]
            for i in range(7,0,-1):
                for j in range(i):
                    W[j]=W[j]-l[i][j]*W[i]
                    H[j]=H[j]-l[i][j]*H[i]
            for m in range(k+2,16):
                Y=V[m]; v=Y; e=E[m]
                for j in range(7,-1,-1):
                    c=lb(Y,8*k+j)
                    v=v-c*W[j]
                    e=e-c*H[j]
                V[m]=v; E[m]=e
    return out


def vmem(*shape):
    return jax.ShapeDtypeStruct(shape, F32)


VMEM = pl.BlockSpec(memory_space=pltpu.VMEM)


def cost(flops, nbytes):
    return pl.CostEstimate(flops=flops, bytes_accessed=nbytes, transcendentals=0)


def aligned(i, n):
    return pl.ds(pl.multiple_of(i * n, n), n)


def call(kernel, out, index, args, flops=0, nbytes=1 << 20, scratch=(), out_specs=None, name=None, limit=12):
    return pl.pallas_call(
        kernel,
        out_shape=out,
        in_specs=[pl.BlockSpec(memory_space=pltpu.SMEM)] + [VMEM] * len(args),
        out_specs=out_specs or jax.tree.map(lambda _: VMEM, out),
        scratch_shapes=list(scratch),
        compiler_params=pltpu.CompilerParams(vmem_limit_bytes=limit << 20),
        cost_estimate=cost(flops, nbytes),
        name=name,
    )(index, *args)


def mask_kernel(limits, x_ref, out):
    live = lax.broadcasted_iota(jnp.int32, out.shape, 0) < limits[1]
    out[...] = jnp.where(live, x_ref[...], 0.0)


def pack_kernel(limits, x_ref, other_ref, out):
    live = lax.broadcasted_iota(jnp.int32, other_ref.shape, 0) < limits[1]
    lead = jnp.where(limits[0] == 0, x_ref[:, :LEAD], jnp.where(live, other_ref[...], 0.0))
    for p in range(8):
        out[p, :, :LEAD] = lead
        out[p, :, LEAD:] = x_ref[:, 256 * p : 256 * p + 256]


def gram_kernel(index, x_ref, out, right):
    right[:, :256] = x_ref[:, LEAD:]
    right[:, 256:] = x_ref[:, aligned(index[0], 256)]
    gram = mtm(x_ref[:, :LEAD], right[...])
    for p in range(8):
        out[p, :64, :] = gram[64 * p : 64 * p + 64, :256]
        out[p, 64:, :] = gram[64 * p : 64 * p + 64, 256:]


def panels(first, d, a, o_ref):
    sub = lax.broadcasted_iota(jnp.int32, S8, 0)
    lane = lax.broadcasted_iota(jnp.int32, S8, 1)
    base = 128 * first
    d[...] = a[0:128, 0:128]

    @pl.loop(0, 2)
    def _(p):
        blocks = chol_inv_128([d[8 * i : 8 * i + 8, :] for i in range(16)], sub, lane)
        for i, block in enumerate(blocks):
            d[8 * i : 8 * i + 8, :] = block
        for q in range(2):

            @pl.when(p == q)
            def _():
                lo, hi = 128 * q, 128 * (q + 1)
                glo, ghi = base + lo, base + hi
                linv = d[...]
                if ghi < LEAD:
                    up = mm(linv, a[lo:hi, hi:])
                    left = a[hi:, hi:] - mtm(up, up)
                    a[hi:, hi:] = left
                    d[...] = left[:128, :128]
                o_ref[glo:ghi, glo:ghi] = linv
                if glo > 0:
                    o_ref[glo:ghi, :glo] = mm(linv, o_ref[glo:ghi, :glo])
                if ghi < LEAD:
                    o_ref[ghi:, :ghi] = o_ref[ghi:, :ghi] - mtm(up, o_ref[glo:ghi, :ghi])


def first_kernel(index, own, other, o_ref, left_ref, token, a, d):
    a[:, aligned(index[0], 256)] = own[...]
    a[:, aligned(1 - index[0], 256)] = other[...]
    o_ref[...] = jnp.zeros_like(o_ref)
    panels(0, d, a, o_ref)
    left_ref[...] = a[256:, 256:]
    token[...] = jnp.zeros_like(token)


def two(x):
    high = x.astype(jnp.bfloat16)
    return high, (x - high.astype(F32)).astype(jnp.bfloat16)


def second_kernel(index, half_ref, left_ref, high_ref, low_ref, o, a, d):
    o[...] = half_ref[...]
    a[...] = left_ref[...]
    panels(2, d, a, o)
    high_ref[...], low_ref[...] = two(o[...])


def product_kernel(index, lh_ref, ll_ref, *refs):
    parts, (out_ref, buf, sems) = refs[:8], refs[8:]
    dot = lambda x, y: jnp.dot(x, y, preferred_element_type=F32)
    copies = []
    for m in range(8):
        xh, xl = two(parts[m][...])
        for r, n in ((0, 256), (256, 512)):
            lh, ll = lh_ref[r : r + 256, :n], ll_ref[r : r + 256, :n]
            y = dot(lh, xh[:n]) + (dot(lh, xl[:n]) + dot(ll, xh[:n]))
            ids = index[0] * 2048 + (index[1] ^ m) * 256 + lax.broadcasted_iota(jnp.int32, y.shape, 1)
            y = jnp.where(ids >= r + lax.broadcasted_iota(jnp.int32, y.shape, 0), y, 0.0)
            buf[m, r : r + 256, :] = y
        copies.append(pltpu.make_async_copy(buf.at[m], out_ref.at[:, aligned(index[1] ^ m, 256)], sems.at[m]))
        copies[-1].start()
    for copy in copies:
        copy.wait()


def cubes(kind):
    groups = {}
    for chip in range(64):
        for core in range(2):
            inside = outside = 0
            for axis, at in enumerate((chip % 4, chip // 4 % 4, chip // 16)):
                bits = (at // 2 ^ at % 2, at // 2)
                first = kind ^ core ^ (axis == 1)
                inside += bits[first] << axis
                outside += bits[1 - first] << axis
            groups.setdefault((core, outside), {})[inside] = chip * 2 + core
    return [[group[i] for i in range(8)] for _, group in sorted(groups.items())]


PLUS, MINUS = cubes(0), cubes(1)


def flip(mask):
    return [(group[i], group[i ^ mask]) for group in PLUS for i in range(8)]


def exchange(x, groups):
    return lax.all_to_all(x, ("row", "col"), 0, 0, axis_index_groups=groups)


def body(contributions, valid_rows):
    blocks, height, width = contributions.shape
    core = lax.axis_index("col")
    row = lax.axis_index("row")
    index = core.reshape(1)

    def across(x):
        return lax.ppermute(x, "col", [(0, 1), (1, 0)])

    def copies(x):
        return jnp.broadcast_to(x[None], (8, *x.shape))

    raw = contributions.reshape(blocks * height, width)
    limits = jnp.stack([core, valid_rows[0]])
    other = across(raw[:, :LEAD])
    masked = call(mask_kernel, vmem(height, width), limits, (raw,), name="mask")
    packed = call(pack_kernel, vmem(8, 128, 768), limits, (masked, other), name="pack")
    packed = exchange(packed, PLUS)
    grams = call(gram_kernel, vmem(8, 128, 256), index, (packed.reshape(1024, 768),), 1 << 30, 4 << 20, (pltpu.VMEM((1024, LEAD), F32),), name="gram", limit=24)
    mine = jnp.sum(exchange(grams, MINUS), axis=0)
    whole = exchange(copies(mine), MINUS)
    rest, square = whole[:, :64].reshape(LEAD, 256), whole[:, 64:].reshape(LEAD, 256)
    def swap(x, mask):
        return lax.ppermute(x, ("row", "col"), flip(mask))

    near = [swap(rest, mask) for mask in (1, 2, 4)]
    far = swap(rest, 7)
    out = (vmem(LEAD, LEAD), vmem(256, 256), vmem(1, 256))
    scratch = (pltpu.VMEM((LEAD, LEAD), F32), pltpu.VMEM((128, 128), F32))
    half, left, zero = call(first_kernel, out, index, (square, across(square)), 10**10, 2 << 20, scratch, name="first")
    scratch = (pltpu.VMEM((LEAD, LEAD), F32), pltpu.VMEM((256, 256), F32), pltpu.VMEM((128, 128), F32))
    out = (jax.ShapeDtypeStruct((LEAD, LEAD), jnp.bfloat16),) * 2
    inverse = call(second_kernel, out, index, (half, left), 10**10, 2 << 20, scratch, name="second")
    x, y, z = (block + zero for block in near)
    xy, yz, zx = swap(y, 1), swap(z, 2), swap(x, 4)
    parts = (rest, near[0], near[1], xy, near[2], zx, yz, far)
    place = 0
    for axis, at in enumerate((row % 4, row // 4 % 4, row // 16)):
        high, gray = at // 2, at // 2 ^ at % 2
        place += jnp.where((core ^ int(axis == 1)) == 0, gray, high) << axis
    index = jnp.stack([core, place]).astype(jnp.int32)
    scratch = (
        pltpu.VMEM((8, LEAD, 256), F32),
        pltpu.SemaphoreType.DMA((8,)),
    )
    spec = pl.BlockSpec(memory_space=pl.ANY)
    return call(product_kernel, vmem(LEAD, width), index, (*inverse, *parts), 3 << 30, 9 << 20, scratch, spec, "product", 24)


def solution(mesh):
    return jax.shard_map(
        body,
        mesh=mesh,
        in_specs=(P(("front", "row"), None, "col"), P(("front", "row"))),
        out_specs=P("front", "col"),
        check_vma=False,
    )
```

```python
import jax
import jax.numpy as jnp
from jax import lax
from jax.experimental import pallas as pl
from jax.experimental.pallas import tpu as pltpu
from jax.sharding import PartitionSpec as P

LEAD = 512
HI = lax.Precision.HIGHEST


S8 = (8, 128)
F32 = jnp.float32
LEFT = (((0,), (0,)), ((), ()))


def lb(x, c):
    return jnp.broadcast_to(x[:, c : c + 1], S8)


def sb(x, j):
    return jnp.broadcast_to(x[j : j + 1, :], S8)


def mm(x, y):
    return jnp.dot(x, y, precision=HI, preferred_element_type=F32)


def mtm(x, y):
    return lax.dot_general(x, y, LEFT, precision=HI, preferred_element_type=F32)


def chol_inv_128(V, sub, lane):
    V=list(V)
    E=[jnp.where(lane==sub+8*k,1.0,0.0) for k in range(16)]
    out=[]
    for k in range(16):
        X=V[k]
        LB=[lb(X,8*k+j) for j in range(8)]
        S=[[sb(LB[j],i) if i>=j else None for j in range(8)] for i in range(8)]
        R=[sb(X,j) for j in range(8)]
        F=[sb(E[k],j) for j in range(8)]
        l=[[None]*8 for _ in range(8)]
        inv=[None]*8
        if k<15:
            Y1=V[k+1]
            C=[lb(Y1,8*k+j) for j in range(8)]
            v1=Y1; e1=E[k+1]
        for j in range(0,8,2):
            a,b,c=S[j][j],S[j+1][j],S[j+1][j+1]
            det=a*c-b*b
            both=1.0/det
            inv[j]=1.0/a
            inv[j+1]=a*both
            l[j+1][j]=b*inv[j]
            S[j+1][j+1]=det*inv[j]
            p={i:S[i][j] for i in range(j+2,8)}
            q={i:S[i][j+1] for i in range(j+2,8)}
            r={}
            near={}
            for i in range(j+2,min(j+4,8)):
                for m in range(j+2,i+1):
                    n=(c*p[i])*p[m]-b*(p[i]*q[m]+q[i]*p[m])+(a*q[i])*q[m] if i!=m else (c*p[i])*p[i]-(b+b)*(p[i]*q[i])+(a*q[i])*q[i]
                    near[i,m]=S[i][m]-n*both
            for i in range(j+2,8):
                l[i][j]=p[i]*inv[j]
                r[i]=q[i]-l[i][j]*b
                l[i][j+1]=r[i]*inv[j+1]
                for m in range(j+2,i+1):
                    S[i][m]=near[i,m] if (i,m) in near else S[i][m]-l[i][j]*p[m]-l[i][j+1]*r[m]
            for t in (j,j+1):
                if k<15:
                    cc=C[t]*inv[t]
                    v1=v1-cc*R[t]
                    e1=e1-cc*F[t]
                    for i in range(t+1,8):
                        C[i]=C[i]-l[i][t]*C[t]
                for i in range(t+1,8):
                    R[i]=R[i]-l[i][t]*R[t]
                    F[i]=F[i]-l[i][t]*F[t]
        o=F[0]*lax.rsqrt(S[0][0])
        for j in range(1,8):
            o=jnp.where(sub==j,F[j]*lax.rsqrt(S[j][j]),o)
        out.append(o)
        if k<15:
            V[k+1]=v1; E[k+1]=e1
        if k<14:
            W=[R[j]*inv[j] for j in range(8)]
            H=[F[j]*inv[j] for j in range(8)]
            for i in range(7,0,-1):
                for j in range(i):
                    W[j]=W[j]-l[i][j]*W[i]
                    H[j]=H[j]-l[i][j]*H[i]
            for m in range(k+2,16):
                Y=V[m]; v=Y; e=E[m]
                for j in range(7,-1,-1):
                    c=lb(Y,8*k+j)
                    v=v-c*W[j]
                    e=e-c*H[j]
                V[m]=v; E[m]=e
    return out


def vmem(*shape):
    return jax.ShapeDtypeStruct(shape, F32)


VMEM = pl.BlockSpec(memory_space=pltpu.VMEM)


def cost(flops, nbytes):
    return pl.CostEstimate(flops=flops, bytes_accessed=nbytes, transcendentals=0)


def aligned(i, n):
    return pl.ds(pl.multiple_of(i * n, n), n)


def call(kernel, out, args, flops=0, nbytes=1 << 20, scratch=(), out_specs=None, name=None, limit=12):
    return pl.pallas_call(
        kernel,
        out_shape=out,
        in_specs=[VMEM] * len(args),
        out_specs=out_specs or jax.tree.map(lambda _: VMEM, out),
        scratch_shapes=list(scratch),
        compiler_params=pltpu.CompilerParams(vmem_limit_bytes=limit << 20),
        cost_estimate=cost(flops, nbytes),
        name=name,
    )(*args)


def two(x):
    high = x.astype(jnp.bfloat16)
    return high, (x - high.astype(F32)).astype(jnp.bfloat16)


def pack_kernel(x_ref, lead_ref, out):
    for p in range(8):
        out[p, :, :LEAD] = lead_ref[...]
        out[p, :, LEAD:] = x_ref[:, 256 * p : 256 * p + 256]


def gram_kernel(x_ref, out, right):
    right[:, :256] = x_ref[:, LEAD:]
    right[:, 256:] = x_ref[:, aligned(lax.axis_index("col"), 256)]
    dot = lambda x, y: lax.dot_general(x, y, LEFT, preferred_element_type=F32)
    xh, xl = two(x_ref[:, :LEAD])
    yh, yl = two(right[...])
    gram = dot(xh, yh) + ((dot(xl, yh) + dot(xh, yl)) + dot(xl, yl))
    for p in range(8):
        out[p, :64, :] = gram[64 * p : 64 * p + 64, :256]
        out[p, 64:, :] = gram[64 * p : 64 * p + 64, 256:]


def panels(first, d, a, o_ref):
    sub = lax.broadcasted_iota(jnp.int32, S8, 0)
    lane = lax.broadcasted_iota(jnp.int32, S8, 1)
    base = 128 * first
    d[...] = a[0:128, 0:128]

    @pl.loop(0, 2)
    def _(p):
        blocks = chol_inv_128([d[8 * i : 8 * i + 8, :] for i in range(16)], sub, lane)
        for i, block in enumerate(blocks):
            d[8 * i : 8 * i + 8, :] = block
        for q in range(2):

            @pl.when(p == q)
            def _():
                lo, hi = 128 * q, 128 * (q + 1)
                glo, ghi = base + lo, base + hi
                linv = d[...]
                if ghi < LEAD:
                    up = mm(linv, a[lo:hi, hi:])
                    left = a[hi:, hi:] - mtm(up, up)
                    a[hi:, hi:] = left
                    d[...] = left[:128, :128]
                o_ref[glo:ghi, glo:ghi] = linv
                if glo > 0:
                    o_ref[glo:ghi, :glo] = mm(linv, o_ref[glo:ghi, :glo])
                if ghi < LEAD:
                    o_ref[ghi:, :ghi] = o_ref[ghi:, :ghi] - mtm(up, o_ref[glo:ghi, :ghi])


def first_kernel(own, other, o_ref, left_ref, token, a, d):
    core = lax.axis_index("col")
    a[:, aligned(core, 256)] = own[...]
    a[:, aligned(1 - core, 256)] = other[...]
    o_ref[...] = jnp.zeros_like(o_ref)
    panels(0, d, a, o_ref)
    left_ref[...] = a[256:, 256:]
    token[...] = jnp.zeros_like(token)


def second_kernel(half_ref, left_ref, head_ref, tail_ref, o, a, d):
    o[...] = half_ref[...]
    a[...] = left_ref[...]
    panels(2, d, a, o)
    head_ref[:LEAD, :], head_ref[LEAD:, :] = two(o[:, :256])
    tail_ref[:256, :], tail_ref[256:, :] = two(o[256:, 256:])


def place():
    core, row = lax.axis_index("col"), lax.axis_index("row")
    x, y, z = row & 3, (row >> 2) & 3, row >> 4
    gray = lambda at: (at >> 1) ^ (at & 1)
    first = gray(x) | ((y >> 1) << 1) | (gray(z) << 2)
    second = (x >> 1) | (gray(y) << 1) | ((z >> 1) << 2)
    return jnp.where(core == 0, first, second)


def product_kernel(head_ref, tail_ref, *refs):
    parts, (out_ref, buf, sems) = refs[:8], refs[8:]
    mine = place()
    offset = lax.axis_index("col") * 2048
    dot = lambda x, y: jnp.dot(x, y, preferred_element_type=F32)
    copies = []
    for m, part in enumerate(parts):
        xh, xl = two(part[:256])
        both = dot(head_ref[...], xh)
        y = both[:LEAD] + (both[LEAD:] + dot(head_ref[:LEAD], xl))
        xh, xl = two(part[256:])
        both = dot(tail_ref[...], xh)
        low = y[256:] + (both[:256] + (both[256:] + dot(tail_ref[:256], xl)))
        column = offset + (mine ^ m) * 256
        for r, block in ((0, y[:256]), (256, low)):
            ids = column + lax.broadcasted_iota(jnp.int32, block.shape, 1)
            buf[m, r : r + 256, :] = jnp.where(ids >= r + lax.broadcasted_iota(jnp.int32, block.shape, 0), block, 0.0)
        copies.append(pltpu.make_async_copy(buf.at[m], out_ref.at[:, aligned(mine ^ m, 256)], sems.at[m]))
        copies[-1].start()
    for copy in copies:
        copy.wait()


def cubes(kind):
    groups = {}
    for chip in range(64):
        for core in range(2):
            inside = outside = 0
            for axis, at in enumerate((chip % 4, chip // 4 % 4, chip // 16)):
                bits = (at // 2 ^ at % 2, at // 2)
                first = kind ^ core ^ (axis == 1)
                inside += bits[first] << axis
                outside += bits[1 - first] << axis
            groups.setdefault((core, outside), {})[inside] = chip * 2 + core
    return [[group[i] for i in range(8)] for _, group in sorted(groups.items())]


PLUS, MINUS = cubes(0), cubes(1)


def flip(mask):
    return [(group[i], group[i ^ mask]) for group in PLUS for i in range(8)]


def exchange(x, groups):
    return lax.all_to_all(x, ("row", "col"), 0, 0, axis_index_groups=groups)


def body(contributions, valid_rows):
    blocks, height, width = contributions.shape
    core = lax.axis_index("col")

    def across(x):
        return lax.ppermute(x, "col", [(0, 1), (1, 0)])

    def copies(x):
        return jnp.broadcast_to(x[None], (8, *x.shape))

    def swap(x, mask):
        return lax.ppermute(x, ("row", "col"), flip(mask))

    raw = contributions.reshape(blocks * height, width)
    other = across(raw[:, :LEAD])
    live = jnp.arange(height, dtype=jnp.int32)[:, None] < valid_rows[0]
    masked = jnp.where(live, raw, 0.0)
    lead = jnp.where(live, jnp.where(core == 0, raw[:, :LEAD], other), 0.0)
    packed = exchange(call(pack_kernel, vmem(8, 128, 768), (masked, lead), name="pack"), PLUS)
    scratch = (pltpu.VMEM((1024, LEAD), F32),)
    grams = call(gram_kernel, vmem(8, 128, 256), (packed.reshape(1024, 768),), 1 << 30, 4 << 20, scratch, name="gram", limit=24)
    mine = jnp.sum(exchange(grams, MINUS), axis=0)
    whole = exchange(copies(mine), MINUS)
    rest, square = whole[:, :64].reshape(LEAD, 256), whole[:, 64:].reshape(LEAD, 256)

    near = [swap(rest, mask) for mask in (1, 2, 4)]
    far = swap(rest, 7)
    out = (vmem(LEAD, LEAD), vmem(256, 256), vmem(1, 256))
    scratch = (pltpu.VMEM((LEAD, LEAD), F32), pltpu.VMEM((128, 128), F32))
    half, left, zero = call(first_kernel, out, (square, across(square)), 10**10, 2 << 20, scratch, name="first")
    scratch = (pltpu.VMEM((LEAD, LEAD), F32), pltpu.VMEM((256, 256), F32), pltpu.VMEM((128, 128), F32))
    out = (jax.ShapeDtypeStruct((2 * LEAD, 256), jnp.bfloat16), jax.ShapeDtypeStruct((LEAD, 256), jnp.bfloat16))
    inverse = call(second_kernel, out, (half, left), 10**10, 2 << 20, scratch, name="second")
    x, y, z = (block + zero for block in near)
    xy, yz, zx = swap(y, 1), swap(z, 2), swap(x, 4)
    parts = (rest, near[0], near[1], xy, near[2], zx, yz, far)
    scratch = (pltpu.VMEM((8, LEAD, 256), F32), pltpu.SemaphoreType.DMA((8,)))
    spec = pl.BlockSpec(memory_space=pl.ANY)
    return call(product_kernel, vmem(LEAD, width), (*inverse, *parts), 3 << 30, 9 << 20, scratch, spec, "product", 24)


def solution(mesh):
    return jax.shard_map(
        body,
        mesh=mesh,
        in_specs=(P(("front", "row"), None, "col"), P(("front", "row"))),
        out_specs=P("front", "col"),
        check_vma=False,
    )
```

```python
import jax
import jax.numpy as jnp
from jax import lax
from jax.experimental import pallas as pl
from jax.experimental.pallas import tpu as pltpu
from jax.sharding import PartitionSpec as P

LEAD = 512
HI = lax.Precision.HIGHEST


S8 = (8, 128)
F32 = jnp.float32
LEFT = (((0,), (0,)), ((), ()))


def lb(x, c):
    return jnp.broadcast_to(x[:, c : c + 1], S8)


def sb(x, j):
    return jnp.broadcast_to(x[j : j + 1, :], S8)


def mm(x, y):
    return jnp.dot(x, y, precision=HI, preferred_element_type=F32)


def mtm(x, y):
    return lax.dot_general(x, y, LEFT, precision=HI, preferred_element_type=F32)


def chol_inv_128(V, sub, lane, u):
    V=list(V)
    E=[jnp.where(lane==sub+8*k,1.0,0.0) for k in range(16)]
    out=[]
    for k in range(16):
        X=V[k]
        u[8*k:8*k+8,:]=X
        R=[u[pl.ds(8*k+j,8,stride=0),:] for j in range(8)]
        S=[[lb(R[i],8*k+j) if i>=j else None for j in range(8)] for i in range(8)]
        u[128+8*k:136+8*k,:]=E[k]
        F=[u[pl.ds(128+8*k+j,8,stride=0),:] for j in range(8)]
        l=[[None]*8 for _ in range(8)]
        inv=[None]*8
        if k<15:
            Y1=V[k+1]
            C=[lb(Y1,8*k+j) for j in range(8)]
            v1=Y1; e1=E[k+1]
        for j in range(0,8,2):
            a,b,c=S[j][j],S[j+1][j],S[j+1][j+1]
            det=a*c-b*b
            both=1.0/det
            inv[j]=1.0/a
            inv[j+1]=a*both
            l[j+1][j]=b*inv[j]
            S[j+1][j+1]=det*inv[j]
            p={i:S[i][j] for i in range(j+2,8)}
            q={i:S[i][j+1] for i in range(j+2,8)}
            r={}
            near={}
            for i in range(j+2,min(j+4,8)):
                for m in range(j+2,i+1):
                    n=(c*p[i])*p[m]-b*(p[i]*q[m]+q[i]*p[m])+(a*q[i])*q[m] if i!=m else (c*p[i])*p[i]-(b+b)*(p[i]*q[i])+(a*q[i])*q[i]
                    near[i,m]=S[i][m]-n*both
            for i in range(j+2,8):
                l[i][j]=p[i]*inv[j]
                r[i]=q[i]-l[i][j]*b
                l[i][j+1]=r[i]*inv[j+1]
                for m in range(j+2,i+1):
                    S[i][m]=near[i,m] if (i,m) in near else S[i][m]-l[i][j]*p[m]-l[i][j+1]*r[m]
            for t in (j,j+1):
                if k<15:
                    cc=C[t]*inv[t]
                    v1=v1-cc*R[t]
                    e1=e1-cc*F[t]
                    for i in range(t+1,8):
                        C[i]=C[i]-l[i][t]*C[t]
                for i in range(t+1,8):
                    R[i]=R[i]-l[i][t]*R[t]
                    F[i]=F[i]-l[i][t]*F[t]
        o=F[0]*lax.rsqrt(S[0][0])
        for j in range(1,8):
            o=jnp.where(sub==j,F[j]*lax.rsqrt(S[j][j]),o)
        out.append(o)
        if k<15:
            V[k+1]=v1; E[k+1]=e1
        if k<14:
            W=[R[j]*inv[j] for j in range(8)]
            H=[F[j]*inv[j] for j in range(8)]
            for i in range(7,0,-1):
                for j in range(i):
                    W[j]=W[j]-l[i][j]*W[i]
                    H[j]=H[j]-l[i][j]*H[i]
            for m in range(k+2,16):
                Y=V[m]; v=Y; e=E[m]
                for j in range(7,-1,-1):
                    c=lb(Y,8*k+j)
                    v=v-c*W[j]
                    e=e-c*H[j]
                V[m]=v; E[m]=e
    return out


def vmem(*shape):
    return jax.ShapeDtypeStruct(shape, F32)


VMEM = pl.BlockSpec(memory_space=pltpu.VMEM)


def cost(flops, nbytes):
    return pl.CostEstimate(flops=flops, bytes_accessed=nbytes, transcendentals=0)


def aligned(i, n):
    return pl.ds(pl.multiple_of(i * n, n), n)


def call(kernel, out, args, flops=0, nbytes=1 << 20, scratch=(), out_specs=None, name=None, limit=12):
    return pl.pallas_call(
        kernel,
        out_shape=out,
        in_specs=[VMEM] * len(args),
        out_specs=out_specs or jax.tree.map(lambda _: VMEM, out),
        scratch_shapes=list(scratch),
        compiler_params=pltpu.CompilerParams(vmem_limit_bytes=limit << 20),
        cost_estimate=cost(flops, nbytes),
        name=name,
    )(*args)


def two(x):
    high = x.astype(jnp.bfloat16)
    return high, (x - high.astype(F32)).astype(jnp.bfloat16)


def pack_kernel(x_ref, lead_ref, out):
    for p in range(8):
        out[p, :, :LEAD] = lead_ref[...]
        out[p, :, LEAD:] = x_ref[:, 256 * p : 256 * p + 256]


def gram_kernel(x_ref, out, right):
    right[:, :256] = x_ref[:, LEAD:]
    right[:, 256:] = x_ref[:, aligned(lax.axis_index("col"), 256)]
    dot = lambda x, y: lax.dot_general(x, y, LEFT, preferred_element_type=F32)
    xh, xl = two(x_ref[:, :LEAD])
    yh, yl = two(right[...])
    gram = dot(xh, yh) + ((dot(xl, yh) + dot(xh, yl)) + dot(xl, yl))
    for p in range(8):
        out[p, :64, :] = gram[64 * p : 64 * p + 64, :256]
        out[p, 64:, :] = gram[64 * p : 64 * p + 64, 256:]


def panels(first, d, a, o_ref, rows):
    sub = lax.broadcasted_iota(jnp.int32, S8, 0)
    lane = lax.broadcasted_iota(jnp.int32, S8, 1)
    base = 128 * first
    d[...] = a[0:128, 0:128]

    @pl.loop(0, 2)
    def _(p):
        blocks = chol_inv_128([d[8 * i : 8 * i + 8, :] for i in range(16)], sub, lane, rows)
        for i, block in enumerate(blocks):
            d[8 * i : 8 * i + 8, :] = block
        for q in range(2):

            @pl.when(p == q)
            def _():
                lo, hi = 128 * q, 128 * (q + 1)
                glo, ghi = base + lo, base + hi
                linv = d[...]
                if ghi < LEAD:
                    up = mm(linv, a[lo:hi, hi:])
                    left = a[hi:, hi:] - mtm(up, up)
                    a[hi:, hi:] = left
                    d[...] = left[:128, :128]
                o_ref[glo:ghi, glo:ghi] = linv
                if glo > 0:
                    o_ref[glo:ghi, :glo] = mm(linv, o_ref[glo:ghi, :glo])
                if ghi < LEAD:
                    o_ref[ghi:, :ghi] = o_ref[ghi:, :ghi] - mtm(up, o_ref[glo:ghi, :ghi])


def first_kernel(own, other, o_ref, left_ref, token, a, d, rows):
    core = lax.axis_index("col")
    a[:, aligned(core, 256)] = own[...]
    a[:, aligned(1 - core, 256)] = other[...]
    o_ref[...] = jnp.zeros_like(o_ref)
    panels(0, d, a, o_ref, rows)
    left_ref[...] = a[256:, 256:]
    token[...] = jnp.zeros_like(token)


def second_kernel(half_ref, left_ref, head_ref, tail_ref, o, a, d, rows):
    o[...] = half_ref[...]
    a[...] = left_ref[...]
    panels(2, d, a, o, rows)
    head_ref[:LEAD, :], head_ref[LEAD:, :] = two(o[:, :256])
    tail_ref[:256, :], tail_ref[256:, :] = two(o[256:, 256:])


def place():
    core, row = lax.axis_index("col"), lax.axis_index("row")
    x, y, z = row & 3, (row >> 2) & 3, row >> 4
    gray = lambda at: (at >> 1) ^ (at & 1)
    first = gray(x) | ((y >> 1) << 1) | (gray(z) << 2)
    second = (x >> 1) | (gray(y) << 1) | ((z >> 1) << 2)
    return jnp.where(core == 0, first, second)


def product_kernel(head_ref, tail_ref, *refs):
    parts, (out_ref, buf, sems) = refs[:8], refs[8:]
    mine = place()
    offset = lax.axis_index("col") * 2048
    dot = lambda x, y: jnp.dot(x, y, preferred_element_type=F32)
    copies = []
    for m, part in enumerate(parts):
        xh, xl = two(part[:256])
        both = dot(head_ref[...], xh)
        y = both[:LEAD] + (both[LEAD:] + dot(head_ref[:LEAD], xl))
        xh, xl = two(part[256:])
        both = dot(tail_ref[...], xh)
        low = y[256:] + (both[:256] + (both[256:] + dot(tail_ref[:256], xl)))
        column = offset + (mine ^ m) * 256
        for r, block in ((0, y[:256]), (256, low)):
            ids = column + lax.broadcasted_iota(jnp.int32, block.shape, 1)
            buf[m, r : r + 256, :] = jnp.where(ids >= r + lax.broadcasted_iota(jnp.int32, block.shape, 0), block, 0.0)
        copies.append(pltpu.make_async_copy(buf.at[m], out_ref.at[:, aligned(mine ^ m, 256)], sems.at[m]))
        copies[-1].start()
    for copy in copies:
        copy.wait()


def cubes(kind):
    groups = {}
    for chip in range(64):
        for core in range(2):
            inside = outside = 0
            for axis, at in enumerate((chip % 4, chip // 4 % 4, chip // 16)):
                bits = (at // 2 ^ at % 2, at // 2)
                first = kind ^ core ^ (axis == 1)
                inside += bits[first] << axis
                outside += bits[1 - first] << axis
            groups.setdefault((core, outside), {})[inside] = chip * 2 + core
    return [[group[i] for i in range(8)] for _, group in sorted(groups.items())]


PLUS, MINUS = cubes(0), cubes(1)


def flip(mask):
    return [(group[i], group[i ^ mask]) for group in PLUS for i in range(8)]


def exchange(x, groups):
    return lax.all_to_all(x, ("row", "col"), 0, 0, axis_index_groups=groups)


def body(contributions, valid_rows):
    blocks, height, width = contributions.shape
    core = lax.axis_index("col")

    def across(x):
        return lax.ppermute(x, "col", [(0, 1), (1, 0)])

    def copies(x):
        return jnp.broadcast_to(x[None], (8, *x.shape))

    def swap(x, mask):
        return lax.ppermute(x, ("row", "col"), flip(mask))

    raw = contributions.reshape(blocks * height, width)
    other = across(raw[:, :LEAD])
    live = jnp.arange(height, dtype=jnp.int32)[:, None] < valid_rows[0]
    masked = jnp.where(live, raw, 0.0)
    lead = jnp.where(core == 0, masked[:, :LEAD], jnp.where(live, other, 0.0))
    packed = exchange(call(pack_kernel, vmem(8, 128, 768), (masked, lead), name="pack"), PLUS)
    scratch = (pltpu.VMEM((1024, LEAD), F32),)
    grams = call(gram_kernel, vmem(8, 128, 256), (packed.reshape(1024, 768),), 1 << 30, 4 << 20, scratch, name="gram", limit=24)
    mine = jnp.sum(exchange(grams, MINUS), axis=0)
    whole = exchange(copies(mine), MINUS)
    rest, square = whole[:, :64].reshape(LEAD, 256), whole[:, 64:].reshape(LEAD, 256)

    near = [swap(rest, mask) for mask in (1, 2, 4)]
    far = swap(rest, 7)
    out = (vmem(LEAD, LEAD), vmem(256, 256), vmem(1, 256))
    scratch = (pltpu.VMEM((LEAD, LEAD), F32), pltpu.VMEM((128, 128), F32), pltpu.VMEM((272, 128), F32))
    half, left, zero = call(first_kernel, out, (square, across(square)), 10**10, 2 << 20, scratch, name="first")
    scratch = (pltpu.VMEM((LEAD, LEAD), F32), pltpu.VMEM((256, 256), F32), pltpu.VMEM((128, 128), F32), pltpu.VMEM((272, 128), F32))
    out = (jax.ShapeDtypeStruct((2 * LEAD, 256), jnp.bfloat16), jax.ShapeDtypeStruct((LEAD, 256), jnp.bfloat16))
    inverse = call(second_kernel, out, (half, left), 10**10, 2 << 20, scratch, name="second")
    x, y, z = (block + zero for block in near)
    xy, yz, zx = swap(y, 1), swap(z, 2), swap(x, 4)
    parts = (rest, near[0], near[1], xy, near[2], zx, yz, far)
    scratch = (pltpu.VMEM((8, LEAD, 256), F32), pltpu.SemaphoreType.DMA((8,)))
    spec = pl.BlockSpec(memory_space=pl.ANY)
    return call(product_kernel, vmem(LEAD, width), (*inverse, *parts), 3 << 30, 9 << 20, scratch, spec, "product", 24)


def solution(mesh):
    return jax.shard_map(
        body,
        mesh=mesh,
        in_specs=(P(("front", "row"), None, "col"), P(("front", "row"))),
        out_specs=P("front", "col"),
        check_vma=False,
    )
```

```python
import jax
import jax.numpy as jnp
from jax import lax
from jax.experimental import pallas as pl
from jax.experimental.pallas import tpu as pltpu
from jax.sharding import PartitionSpec as P

LEAD = 512
HI = lax.Precision.HIGHEST


S8 = (8, 128)
F32 = jnp.float32
LEFT = (((0,), (0,)), ((), ()))


def lb(x, c):
    return jnp.broadcast_to(x[:, c : c + 1], S8)


def sb(x, j):
    return jnp.broadcast_to(x[j : j + 1, :], S8)


def mm(x, y):
    return jnp.dot(x, y, precision=HI, preferred_element_type=F32)


def mtm(x, y):
    return lax.dot_general(x, y, LEFT, precision=HI, preferred_element_type=F32)


def chol_inv_128(V, sub, lane, u):
    V=list(V)
    E=[jnp.where(lane==sub+8*k,1.0,0.0) for k in range(16)]
    out=[]
    for k in range(16):
        X=V[k]
        u[8*k:8*k+8,:]=X
        R=[u[pl.ds(8*k+j,8,stride=0),:] for j in range(8)]
        S=[[lb(R[i],8*k+j) if i>=j else None for j in range(8)] for i in range(8)]
        u[128+8*k:136+8*k,:]=E[k]
        F=[u[pl.ds(128+8*k+j,8,stride=0),:] for j in range(8)]
        l=[[None]*8 for _ in range(8)]
        inv=[None]*8
        if k<15:
            Y1=V[k+1]
            C=[lb(Y1,8*k+j) for j in range(8)]
            v1=Y1; e1=E[k+1]
        for j in range(0,8,2):
            a,b,c=S[j][j],S[j+1][j],S[j+1][j+1]
            det=a*c-b*b
            both=1.0/det
            inv[j]=1.0/a
            inv[j+1]=a*both
            l[j+1][j]=b*inv[j]
            S[j+1][j+1]=det*inv[j]
            p={i:S[i][j] for i in range(j+2,8)}
            q={i:S[i][j+1] for i in range(j+2,8)}
            r={}
            near={}
            for i in range(j+2,min(j+4,8)):
                for m in range(j+2,i+1):
                    n=(c*p[i])*p[m]-b*(p[i]*q[m]+q[i]*p[m])+(a*q[i])*q[m] if i!=m else (c*p[i])*p[i]-(b+b)*(p[i]*q[i])+(a*q[i])*q[i]
                    near[i,m]=S[i][m]-n*both
            for i in range(j+2,8):
                l[i][j]=p[i]*inv[j]
                r[i]=q[i]-l[i][j]*b
                l[i][j+1]=r[i]*inv[j+1]
                for m in range(j+2,i+1):
                    S[i][m]=near[i,m] if (i,m) in near else S[i][m]-l[i][j]*p[m]-l[i][j+1]*r[m]
            for t in (j,j+1):
                if k<15:
                    cc=C[t]*inv[t]
                    v1=v1-cc*R[t]
                    e1=e1-cc*F[t]
                    for i in range(t+1,8):
                        C[i]=C[i]-l[i][t]*C[t]
                for i in range(t+1,8):
                    R[i]=R[i]-l[i][t]*R[t]
                    F[i]=F[i]-l[i][t]*F[t]
        o=F[0]*lax.rsqrt(S[0][0])
        for j in range(1,8):
            o=jnp.where(sub==j,F[j]*lax.rsqrt(S[j][j]),o)
        out.append(o)
        if k<15:
            V[k+1]=v1; E[k+1]=e1
        if k<14:
            W=[R[j]*inv[j] for j in range(8)]
            H=[F[j]*inv[j] for j in range(8)]
            for i in range(7,0,-1):
                for j in range(i):
                    W[j]=W[j]-l[i][j]*W[i]
                    H[j]=H[j]-l[i][j]*H[i]
            for m in range(k+2,16):
                Y=V[m]; v=Y; e=E[m]
                for j in range(7,-1,-1):
                    c=lb(Y,8*k+j)
                    v=v-c*W[j]
                    e=e-c*H[j]
                V[m]=v; E[m]=e
    return out


def vmem(*shape):
    return jax.ShapeDtypeStruct(shape, F32)


VMEM = pl.BlockSpec(memory_space=pltpu.VMEM)


def cost(flops, nbytes):
    return pl.CostEstimate(flops=flops, bytes_accessed=nbytes, transcendentals=0)


def aligned(i, n):
    return pl.ds(pl.multiple_of(i * n, n), n)


def call(kernel, out, args, flops=0, nbytes=1 << 20, scratch=(), out_specs=None, name=None, limit=12):
    return pl.pallas_call(
        kernel,
        out_shape=out,
        in_specs=[VMEM] * len(args),
        out_specs=out_specs or jax.tree.map(lambda _: VMEM, out),
        scratch_shapes=list(scratch),
        compiler_params=pltpu.CompilerParams(vmem_limit_bytes=limit << 20),
        cost_estimate=cost(flops, nbytes),
        name=name,
    )(*args)


def two(x):
    high = x.astype(jnp.bfloat16)
    return high, (x - high.astype(F32)).astype(jnp.bfloat16)


def pack_kernel(x_ref, other_ref, valid_ref, out):
    live = lax.broadcasted_iota(jnp.int32, (128, 128), 0) < valid_ref[...]
    clear = lambda x: jnp.concatenate([jnp.where(live, x[:, i : i + 128], 0.0) for i in range(0, x.shape[1], 128)], axis=1)
    lead = clear(jnp.where(lax.axis_index("col") == 0, x_ref[:, :LEAD], other_ref[...]))
    for p in range(8):
        out[p, :, :LEAD] = lead
        out[p, :, LEAD:] = clear(x_ref[:, 256 * p : 256 * p + 256])


def gram_kernel(x_ref, out, right):
    right[:, :256] = x_ref[:, LEAD:]
    right[:, 256:] = x_ref[:, aligned(lax.axis_index("col"), 256)]
    dot = lambda x, y: lax.dot_general(x, y, LEFT, preferred_element_type=F32)
    xh, xl = two(x_ref[:, :LEAD])
    yh, yl = two(right[...])
    gram = dot(xh, yh) + ((dot(xl, yh) + dot(xh, yl)) + dot(xl, yl))
    for p in range(8):
        out[p, :64, :] = gram[64 * p : 64 * p + 64, :256]
        out[p, 64:, :] = gram[64 * p : 64 * p + 64, 256:]


def panels(first, d, a, o_ref, rows):
    sub = lax.broadcasted_iota(jnp.int32, S8, 0)
    lane = lax.broadcasted_iota(jnp.int32, S8, 1)
    base = 128 * first
    d[...] = a[0:128, 0:128]

    @pl.loop(0, 2)
    def _(p):
        blocks = chol_inv_128([d[8 * i : 8 * i + 8, :] for i in range(16)], sub, lane, rows)
        for i, block in enumerate(blocks):
            d[8 * i : 8 * i + 8, :] = block
        for q in range(2):

            @pl.when(p == q)
            def _():
                lo, hi = 128 * q, 128 * (q + 1)
                glo, ghi = base + lo, base + hi
                linv = d[...]
                if ghi < LEAD:
                    up = mm(linv, a[lo:hi, hi:])
                    left = a[hi:, hi:] - mtm(up, up)
                    a[hi:, hi:] = left
                    d[...] = left[:128, :128]
                o_ref[glo:ghi, glo:ghi] = linv
                if glo > 0:
                    o_ref[glo:ghi, :glo] = mm(linv, o_ref[glo:ghi, :glo])
                if ghi < LEAD:
                    o_ref[ghi:, :ghi] = o_ref[ghi:, :ghi] - mtm(up, o_ref[glo:ghi, :ghi])


def first_kernel(own, other, o_ref, left_ref, token, a, d, rows):
    core = lax.axis_index("col")
    a[:, aligned(core, 256)] = own[...]
    a[:, aligned(1 - core, 256)] = other[...]
    o_ref[...] = jnp.zeros_like(o_ref)
    panels(0, d, a, o_ref, rows)
    left_ref[...] = a[256:, 256:]
    token[...] = jnp.zeros_like(token)


def second_kernel(half_ref, left_ref, head_ref, tail_ref, o, a, d, rows):
    o[...] = half_ref[...]
    a[...] = left_ref[...]
    panels(2, d, a, o, rows)
    head_ref[:LEAD, :], head_ref[LEAD:, :] = two(o[:, :256])
    tail_ref[:256, :], tail_ref[256:, :] = two(o[256:, 256:])


def place():
    core, row = lax.axis_index("col"), lax.axis_index("row")
    x, y, z = row & 3, (row >> 2) & 3, row >> 4
    gray = lambda at: (at >> 1) ^ (at & 1)
    first = gray(x) | ((y >> 1) << 1) | (gray(z) << 2)
    second = (x >> 1) | (gray(y) << 1) | ((z >> 1) << 2)
    return jnp.where(core == 1, first, second)


def product_kernel(head_ref, tail_ref, *refs):
    parts, (out_ref, buf, sems) = refs[:8], refs[8:]
    mine = place()
    offset = lax.axis_index("col") * 2048
    dot = lambda x, y: jnp.dot(x, y, preferred_element_type=F32)
    copies = []
    for m, part in enumerate(parts):
        xh, xl = two(part[:256])
        both = dot(head_ref[...], xh)
        y = both[:LEAD] + (both[LEAD:] + dot(head_ref[:LEAD], xl))
        xh, xl = two(part[256:])
        both = dot(tail_ref[...], xh)
        low = y[256:] + (both[:256] + (both[256:] + dot(tail_ref[:256], xl)))
        column = offset + (mine ^ m) * 256
        for r, block in ((0, y[:256]), (256, low)):
            ids = column + lax.broadcasted_iota(jnp.int32, block.shape, 1)
            buf[m, r : r + 256, :] = jnp.where(ids >= r + lax.broadcasted_iota(jnp.int32, block.shape, 0), block, 0.0)
        copies.append(pltpu.make_async_copy(buf.at[m], out_ref.at[:, aligned(mine ^ m, 256)], sems.at[m]))
        copies[-1].start()
    for copy in copies:
        copy.wait()


def cubes(kind):
    groups = {}
    for chip in range(64):
        for core in range(2):
            inside = outside = 0
            for axis, at in enumerate((chip % 4, chip // 4 % 4, chip // 16)):
                bits = (at // 2 ^ at % 2, at // 2)
                first = kind ^ core ^ (axis != 1)
                inside += bits[first] << axis
                outside += bits[1 - first] << axis
            groups.setdefault((core, outside), {})[inside] = chip * 2 + core
    return [[group[i] for i in range(8)] for _, group in sorted(groups.items())]


PLUS, MINUS = cubes(0), cubes(1)


def flip(mask):
    return [(group[i], group[i ^ mask]) for group in PLUS for i in range(8)]


def exchange(x, groups):
    return lax.all_to_all(x, ("row", "col"), 0, 0, axis_index_groups=groups)


def body(contributions, valid_rows):
    blocks, height, width = contributions.shape
    core = lax.axis_index("col")

    def across(x):
        return lax.ppermute(x, "col", [(0, 1), (1, 0)])

    def copies(x):
        return jnp.broadcast_to(x[None], (8, *x.shape))

    def swap(x, mask):
        return lax.ppermute(x, ("row", "col"), flip(mask))

    raw = contributions.reshape(blocks * height, width)
    other = across(raw[:, :LEAD])
    packed = call(pack_kernel, vmem(8, 128, 768), (raw, other, valid_rows.reshape(1, 1)), name="pack")
    packed = exchange(packed, PLUS)
    scratch = (pltpu.VMEM((1024, LEAD), F32),)
    grams = call(gram_kernel, vmem(8, 128, 256), (packed.reshape(1024, 768),), 1 << 30, 4 << 20, scratch, name="gram", limit=24)
    mine = jnp.sum(exchange(grams, MINUS), axis=0)
    whole = exchange(copies(mine), MINUS)
    rest, square = whole[:, :64].reshape(LEAD, 256), whole[:, 64:].reshape(LEAD, 256)

    near = [swap(rest, mask) for mask in (1, 2, 4)]
    far = swap(rest, 7)
    out = (vmem(LEAD, LEAD), vmem(256, 256), vmem(1, 256))
    scratch = (pltpu.VMEM((LEAD, LEAD), F32), pltpu.VMEM((128, 128), F32), pltpu.VMEM((272, 128), F32))
    half, left, zero = call(first_kernel, out, (square, across(square)), 10**10, 2 << 20, scratch, name="first")
    scratch = (pltpu.VMEM((LEAD, LEAD), F32), pltpu.VMEM((256, 256), F32), pltpu.VMEM((128, 128), F32), pltpu.VMEM((272, 128), F32))
    out = (jax.ShapeDtypeStruct((2 * LEAD, 256), jnp.bfloat16), jax.ShapeDtypeStruct((LEAD, 256), jnp.bfloat16))
    inverse = call(second_kernel, out, (half, left), 10**10, 2 << 20, scratch, name="second")
    x, y, z = (block + zero for block in near)
    xy, yz, zx = swap(y, 1), swap(z, 2), swap(x, 4)
    parts = (rest, near[0], near[1], xy, near[2], zx, yz, far)
    scratch = (pltpu.VMEM((8, LEAD, 256), F32), pltpu.SemaphoreType.DMA((8,)))
    spec = pl.BlockSpec(memory_space=pl.ANY)
    return call(product_kernel, vmem(LEAD, width), (*inverse, *parts), 3 << 30, 9 << 20, scratch, spec, "product", 24)


def solution(mesh):
    return jax.shard_map(
        body,
        mesh=mesh,
        in_specs=(P(("front", "row"), None, "col"), P(("front", "row"))),
        out_specs=P("front", "col"),
        check_vma=False,
    )
```

```python
import functools

import jax
import jax.numpy as jnp
from jax import lax
from jax.experimental import pallas as pl
from jax.experimental.pallas import tpu as pltpu
from jax.sharding import PartitionSpec as P

LEAD = 512
HI = lax.Precision.HIGHEST


S8 = (8, 128)
F32 = jnp.float32
LEFT = (((0,), (0,)), ((), ()))


def lb(x, c):
    return jnp.broadcast_to(x[:, c : c + 1], S8)


def sb(x, j):
    return jnp.broadcast_to(x[j : j + 1, :], S8)


def mm(x, y):
    return jnp.dot(x, y, precision=HI, preferred_element_type=F32)


def mtm(x, y):
    return lax.dot_general(x, y, LEFT, precision=HI, preferred_element_type=F32)


def chol_inv_128(V, sub, lane, u):
    V=list(V)
    E=[jnp.where(lane==sub+8*k,1.0,0.0) for k in range(16)]
    out=[]
    for k in range(16):
        X=V[k]
        u[8*k:8*k+8,:]=X
        R=[u[pl.ds(8*k+j,8,stride=0),:] for j in range(8)]
        S=[[lb(R[i],8*k+j) if i>=j else None for j in range(8)] for i in range(8)]
        u[128+8*k:136+8*k,:]=E[k]
        F=[u[pl.ds(128+8*k+j,8,stride=0),:] for j in range(8)]
        l=[[None]*8 for _ in range(8)]
        inv=[None]*8
        if k<15:
            Y1=V[k+1]
            C=[lb(Y1,8*k+j) for j in range(8)]
            v1=Y1; e1=E[k+1]
        for j in range(0,8,2):
            a,b,c=S[j][j],S[j+1][j],S[j+1][j+1]
            det=a*c-b*b
            both=1.0/det
            inv[j]=1.0/a
            inv[j+1]=a*both
            l[j+1][j]=b*inv[j]
            S[j+1][j+1]=det*inv[j]
            p={i:S[i][j] for i in range(j+2,8)}
            q={i:S[i][j+1] for i in range(j+2,8)}
            r={}
            near={}
            for i in range(j+2,min(j+4,8)):
                for m in range(j+2,i+1):
                    n=(c*p[i])*p[m]-b*(p[i]*q[m]+q[i]*p[m])+(a*q[i])*q[m] if i!=m else (c*p[i])*p[i]-(b+b)*(p[i]*q[i])+(a*q[i])*q[i]
                    near[i,m]=S[i][m]-n*both
            for i in range(j+2,8):
                l[i][j]=p[i]*inv[j]
                r[i]=q[i]-l[i][j]*b
                l[i][j+1]=r[i]*inv[j+1]
                for m in range(j+2,i+1):
                    S[i][m]=near[i,m] if (i,m) in near else S[i][m]-l[i][j]*p[m]-l[i][j+1]*r[m]
            for t in (j,j+1):
                if k<15:
                    cc=C[t]*inv[t]
                    v1=v1-cc*R[t]
                    e1=e1-cc*F[t]
                    for i in range(t+1,8):
                        C[i]=C[i]-l[i][t]*C[t]
                for i in range(t+1,8):
                    R[i]=R[i]-l[i][t]*R[t]
                    F[i]=F[i]-l[i][t]*F[t]
        o=F[0]*lax.rsqrt(S[0][0])
        for j in range(1,8):
            o=jnp.where(sub==j,F[j]*lax.rsqrt(S[j][j]),o)
        out.append(o)
        if k<15:
            V[k+1]=v1; E[k+1]=e1
        if k<14:
            W=[R[j]*inv[j] for j in range(8)]
            H=[F[j]*inv[j] for j in range(8)]
            for i in range(7,0,-1):
                for j in range(i):
                    W[j]=W[j]-l[i][j]*W[i]
                    H[j]=H[j]-l[i][j]*H[i]
            for m in range(k+2,16):
                Y=V[m]; v=Y; e=E[m]
                for j in range(7,-1,-1):
                    c=lb(Y,8*k+j)
                    v=v-c*W[j]
                    e=e-c*H[j]
                V[m]=v; E[m]=e
    return out


def vmem(*shape):
    return jax.ShapeDtypeStruct(shape, F32)


VMEM = pl.BlockSpec(memory_space=pltpu.VMEM)


def cost(flops, nbytes):
    return pl.CostEstimate(flops=flops, bytes_accessed=nbytes, transcendentals=0)


def aligned(i, n):
    return pl.ds(pl.multiple_of(i * n, n), n)


def call(kernel, out, args, flops=0, nbytes=1 << 20, scratch=(), out_specs=None, name=None, limit=12):
    return pl.pallas_call(
        kernel,
        out_shape=out,
        in_specs=[VMEM] * len(args),
        out_specs=out_specs or jax.tree.map(lambda _: VMEM, out),
        scratch_shapes=list(scratch),
        compiler_params=pltpu.CompilerParams(vmem_limit_bytes=limit << 20),
        cost_estimate=cost(flops, nbytes),
        name=name,
    )(*args)


def two(x):
    high = x.astype(jnp.bfloat16)
    return high, (x - high.astype(F32)).astype(jnp.bfloat16)


def pack_kernel(x_ref, lead_ref, out):
    for p in range(8):
        out[p, :, :LEAD] = lead_ref[...]
        out[p, :, LEAD:] = x_ref[:, 256 * p : 256 * p + 256]


def gram_kernel(x_ref, out, right):
    right[:, :256] = x_ref[:, LEAD:]
    right[:, 256:] = x_ref[:, aligned(lax.axis_index("col"), 256)]
    dot = lambda x, y: lax.dot_general(x, y, LEFT, preferred_element_type=F32)
    xh, xl = two(x_ref[:, :LEAD])
    yh, yl = two(right[...])
    gram = dot(xh, yh) + ((dot(xl, yh) + dot(xh, yl)) + dot(xl, yl))
    for p in range(8):
        out[p, :64, :] = gram[64 * p : 64 * p + 64, :256]
        out[p, 64:, :] = gram[64 * p : 64 * p + 64, 256:]


def panels(first, d, a, o_ref, rows):
    sub = lax.broadcasted_iota(jnp.int32, S8, 0)
    lane = lax.broadcasted_iota(jnp.int32, S8, 1)
    base = 128 * first
    d[...] = a[0:128, 0:128]

    @pl.loop(0, 2)
    def _(p):
        blocks = chol_inv_128([d[8 * i : 8 * i + 8, :] for i in range(16)], sub, lane, rows)
        for i, block in enumerate(blocks):
            d[8 * i : 8 * i + 8, :] = block
        for q in range(2):

            @pl.when(p == q)
            def _():
                lo, hi = 128 * q, 128 * (q + 1)
                glo, ghi = base + lo, base + hi
                linv = d[...]
                if ghi < LEAD:
                    up = mm(linv, a[lo:hi, hi:])
                    left = a[hi:, hi:] - mtm(up, up)
                    a[hi:, hi:] = left
                    d[...] = left[:128, :128]
                o_ref[glo:ghi, glo:ghi] = linv
                if glo > 0:
                    o_ref[glo:ghi, :glo] = mm(linv, o_ref[glo:ghi, :glo])
                if ghi < LEAD:
                    o_ref[ghi:, :ghi] = o_ref[ghi:, :ghi] - mtm(up, o_ref[glo:ghi, :ghi])


def first_kernel(own, other, o_ref, left_ref, token, a, d, rows):
    core = lax.axis_index("col")
    a[:, aligned(core, 256)] = own[...]
    a[:, aligned(1 - core, 256)] = other[...]
    o_ref[...] = jnp.zeros_like(o_ref)
    panels(0, d, a, o_ref, rows)
    left_ref[...] = a[256:, 256:]
    token[...] = jnp.zeros_like(token)


def second_kernel(half_ref, left_ref, head_ref, tail_ref, o, a, d, rows):
    o[...] = half_ref[...]
    a[...] = left_ref[...]
    panels(2, d, a, o, rows)
    head_ref[:LEAD, :], head_ref[LEAD:, :] = two(o[:, :256])
    tail_ref[:256, :], tail_ref[256:, :] = two(o[256:, 256:])


def place():
    core, row = lax.axis_index("col"), lax.axis_index("row")
    x, y, z = row & 3, (row >> 2) & 3, row >> 4
    gray = lambda at: (at >> 1) ^ (at & 1)
    first = gray(x) | ((y >> 1) << 1) | (gray(z) << 2)
    second = (x >> 1) | (gray(y) << 1) | ((z >> 1) << 2)
    return jnp.where(core == 1, first, second)


def product_kernel(masks, head_ref, tail_ref, *refs):
    parts, (out_ref, buf, sems) = refs[: len(masks)], refs[-3:]
    mine = place()
    offset = lax.axis_index("col") * 2048
    dot = lambda x, y: jnp.dot(x, y, preferred_element_type=F32)
    copies = []
    for i, (m, part) in enumerate(zip(masks, parts)):
        xh, xl = two(part[:256])
        both = dot(head_ref[...], xh)
        y = both[:LEAD] + (both[LEAD:] + dot(head_ref[:LEAD], xl))
        xh, xl = two(part[256:])
        both = dot(tail_ref[...], xh)
        low = y[256:] + (both[:256] + (both[256:] + dot(tail_ref[:256], xl)))
        column = offset + (mine ^ m) * 256
        for r, block in ((0, y[:256]), (256, low)):
            ids = column + lax.broadcasted_iota(jnp.int32, block.shape, 1)
            buf[i, r : r + 256, :] = jnp.where(ids >= r + lax.broadcasted_iota(jnp.int32, block.shape, 0), block, 0.0)
        copies.append(pltpu.make_async_copy(buf.at[i], out_ref.at[:, aligned(mine ^ m, 256)], sems.at[i]))
        copies[-1].start()
    for copy in copies:
        copy.wait()


def product(masks, inverse, parts, out=None):
    n = len(parts)
    hbm = pl.BlockSpec(memory_space=pl.ANY)
    more = () if out is None else (out,)
    return pl.pallas_call(
        functools.partial(product_kernel, masks),
        out_shape=vmem(LEAD, 2048),
        in_specs=[VMEM] * (2 + n) + [hbm] * len(more),
        out_specs=hbm,
        scratch_shapes=[pltpu.VMEM((n, LEAD, 256), F32), pltpu.SemaphoreType.DMA((n,))],
        input_output_aliases={2 + n: 0} if more else {},
        compiler_params=pltpu.CompilerParams(vmem_limit_bytes=24 << 20),
        cost_estimate=cost(n * 400_000_000, n << 20),
        name="product",
    )(*inverse, *parts, *more)


def cubes(kind):
    groups = {}
    for chip in range(64):
        for core in range(2):
            inside = outside = 0
            for axis, at in enumerate((chip % 4, chip // 4 % 4, chip // 16)):
                bits = (at // 2 ^ at % 2, at // 2)
                first = kind ^ core ^ (axis != 1)
                inside += bits[first] << axis
                outside += bits[1 - first] << axis
            groups.setdefault((core, outside), {})[inside] = chip * 2 + core
    return [[group[i] for i in range(8)] for _, group in sorted(groups.items())]


PLUS, MINUS = cubes(0), cubes(1)


def flip(mask):
    return [(group[i], group[i ^ mask]) for group in PLUS for i in range(8)]


def exchange(x, groups):
    return lax.all_to_all(x, ("row", "col"), 0, 0, axis_index_groups=groups)


def body(contributions, valid_rows):
    blocks, height, width = contributions.shape
    core = lax.axis_index("col")

    def across(x):
        return lax.ppermute(x, "col", [(0, 1), (1, 0)])

    def copies(x):
        return jnp.broadcast_to(x[None], (8, *x.shape))

    def swap(x, mask):
        return lax.ppermute(x, ("row", "col"), flip(mask))

    raw = contributions.reshape(blocks * height, width)
    other = across(raw[:, :LEAD])
    live = jnp.arange(height, dtype=jnp.int32)[:, None] < valid_rows[0]
    masked = jnp.where(live, raw, 0.0)
    lead = jnp.where(core == 0, masked[:, :LEAD], jnp.where(live, other, 0.0))
    packed = exchange(call(pack_kernel, vmem(8, 128, 768), (masked, lead), name="pack"), PLUS)
    scratch = (pltpu.VMEM((1024, LEAD), F32),)
    grams = call(gram_kernel, vmem(8, 128, 256), (packed.reshape(1024, 768),), 1 << 30, 4 << 20, scratch, name="gram", limit=24)
    mine = jnp.sum(exchange(grams, MINUS), axis=0)
    whole = exchange(copies(mine), MINUS)
    rest, square = whole[:, :64].reshape(LEAD, 256), whole[:, 64:].reshape(LEAD, 256)

    near = [swap(rest, mask) for mask in (1, 2, 4)]
    far = swap(rest, 7)
    out = (vmem(LEAD, LEAD), vmem(256, 256), vmem(1, 256))
    scratch = (pltpu.VMEM((LEAD, LEAD), F32), pltpu.VMEM((128, 128), F32), pltpu.VMEM((272, 128), F32))
    half, left, zero = call(first_kernel, out, (square, across(square)), 10**10, 2 << 20, scratch, name="first")
    scratch = (pltpu.VMEM((LEAD, LEAD), F32), pltpu.VMEM((256, 256), F32), pltpu.VMEM((128, 128), F32), pltpu.VMEM((272, 128), F32))
    out = (jax.ShapeDtypeStruct((2 * LEAD, 256), jnp.bfloat16), jax.ShapeDtypeStruct((LEAD, 256), jnp.bfloat16))
    inverse = call(second_kernel, out, (half, left), 10**10, 2 << 20, scratch, name="second")
    x, y, z = (block + zero for block in near)
    xy, yz, zx = swap(y, 1), swap(z, 2), swap(x, 4)
    done = product((0, 1, 2, 4, 7), inverse, (rest, *near, far))
    return product((3, 6, 5), inverse, (xy, yz, zx), done)


def solution(mesh):
    return jax.shard_map(
        body,
        mesh=mesh,
        in_specs=(P(("front", "row"), None, "col"), P(("front", "row"))),
        out_specs=P("front", "col"),
        check_vma=False,
    )
```

```python
import functools

import jax
import jax.numpy as jnp
from jax import lax
from jax.experimental import pallas as pl
from jax.experimental.pallas import tpu as pltpu
from jax.sharding import PartitionSpec as P

LEAD = 512
HI = lax.Precision.HIGHEST


S8 = (8, 128)
F32 = jnp.float32
LEFT = (((0,), (0,)), ((), ()))


def lb(x, c):
    return jnp.broadcast_to(x[:, c : c + 1], S8)


def sb(x, j):
    return jnp.broadcast_to(x[j : j + 1, :], S8)


def mm(x, y):
    return jnp.dot(x, y, precision=HI, preferred_element_type=F32)


def mtm(x, y):
    return lax.dot_general(x, y, LEFT, precision=HI, preferred_element_type=F32)


def chol_inv_128(V, sub, lane, u):
    V=list(V)
    E=[jnp.where(lane==sub+8*k,1.0,0.0) for k in range(16)]
    out=[]
    for k in range(16):
        X=V[k]
        u[8*k:8*k+8,:]=X
        R=[u[pl.ds(8*k+j,8,stride=0),:] for j in range(8)]
        for j in range(8): u[256+8*j:264+8*j,:]=lb(X,8*k+j)
        S=[[u[pl.ds(256+8*j+i,8,stride=0),:] if i>=j else None for j in range(8)] for i in range(8)]
        u[128+8*k:136+8*k,:]=E[k]
        F=[u[pl.ds(128+8*k+j,8,stride=0),:] for j in range(8)]
        l=[[None]*8 for _ in range(8)]
        inv=[None]*8
        if k<15:
            Y1=V[k+1]
            C=[lb(Y1,8*k+j) for j in range(8)]
            v1=Y1; e1=E[k+1]
        for j in range(0,8,2):
            a,b,c=S[j][j],S[j+1][j],S[j+1][j+1]
            det=a*c-b*b
            both=1.0/det
            inv[j]=1.0/a
            inv[j+1]=a*both
            l[j+1][j]=b*inv[j]
            S[j+1][j+1]=det*inv[j]
            p={i:S[i][j] for i in range(j+2,8)}
            q={i:S[i][j+1] for i in range(j+2,8)}
            r={}
            near={}
            for i in range(j+2,min(j+4,8)):
                for m in range(j+2,i+1):
                    n=(c*p[i])*p[m]-b*(p[i]*q[m]+q[i]*p[m])+(a*q[i])*q[m] if i!=m else (c*p[i])*p[i]-(b+b)*(p[i]*q[i])+(a*q[i])*q[i]
                    near[i,m]=S[i][m]-n*both
            for i in range(j+2,8):
                l[i][j]=p[i]*inv[j]
                r[i]=q[i]-l[i][j]*b
                l[i][j+1]=r[i]*inv[j+1]
                for m in range(j+2,i+1):
                    S[i][m]=near[i,m] if (i,m) in near else S[i][m]-l[i][j]*p[m]-l[i][j+1]*r[m]
            for t in (j,j+1):
                if k<15:
                    cc=C[t]*inv[t]
                    v1=v1-cc*R[t]
                    e1=e1-cc*F[t]
                    for i in range(t+1,8):
                        C[i]=C[i]-l[i][t]*C[t]
                for i in range(t+1,8):
                    R[i]=R[i]-l[i][t]*R[t]
                    F[i]=F[i]-l[i][t]*F[t]
        o=F[0]*lax.rsqrt(S[0][0])
        for j in range(1,8):
            o=jnp.where(sub==j,F[j]*lax.rsqrt(S[j][j]),o)
        out.append(o)
        if k<15:
            V[k+1]=v1; E[k+1]=e1
        if k<14:
            W=[R[j]*inv[j] for j in range(8)]
            H=[F[j]*inv[j] for j in range(8)]
            for i in range(7,0,-1):
                for j in range(i):
                    W[j]=W[j]-l[i][j]*W[i]
                    H[j]=H[j]-l[i][j]*H[i]
            for m in range(k+2,16):
                Y=V[m]; v=Y; e=E[m]
                for j in range(7,-1,-1):
                    c=lb(Y,8*k+j)
                    v=v-c*W[j]
                    e=e-c*H[j]
                V[m]=v; E[m]=e
    return out


def vmem(*shape):
    return jax.ShapeDtypeStruct(shape, F32)


VMEM = pl.BlockSpec(memory_space=pltpu.VMEM)


def cost(flops, nbytes):
    return pl.CostEstimate(flops=flops, bytes_accessed=nbytes, transcendentals=0)


def aligned(i, n):
    return pl.ds(pl.multiple_of(i * n, n), n)


def call(kernel, out, args, flops=0, nbytes=1 << 20, scratch=(), out_specs=None, name=None, limit=12):
    return pl.pallas_call(
        kernel,
        out_shape=out,
        in_specs=[VMEM] * len(args),
        out_specs=out_specs or jax.tree.map(lambda _: VMEM, out),
        scratch_shapes=list(scratch),
        compiler_params=pltpu.CompilerParams(vmem_limit_bytes=limit << 20),
        cost_estimate=cost(flops, nbytes),
        name=name,
    )(*args)


def two(x):
    high = x.astype(jnp.bfloat16)
    return high, (x - high.astype(F32)).astype(jnp.bfloat16)


def pack_kernel(x_ref, lead_ref, out):
    for p in range(8):
        out[p, :, :LEAD] = lead_ref[...]
        out[p, :, LEAD:] = x_ref[:, 256 * p : 256 * p + 256]


def gram_kernel(x_ref, out, right):
    right[:, :256] = x_ref[:, LEAD:]
    right[:, 256:] = x_ref[:, aligned(lax.axis_index("col"), 256)]
    dot = lambda x, y: lax.dot_general(x, y, LEFT, preferred_element_type=F32)
    xh, xl = two(x_ref[:, :LEAD])
    yh, yl = two(right[...])
    gram = dot(xh, yh) + ((dot(xl, yh) + dot(xh, yl)) + dot(xl, yl))
    for p in range(8):
        out[p, :64, :] = gram[64 * p : 64 * p + 64, :256]
        out[p, 64:, :] = gram[64 * p : 64 * p + 64, 256:]


def panels(first, d, a, o_ref, rows):
    sub = lax.broadcasted_iota(jnp.int32, S8, 0)
    lane = lax.broadcasted_iota(jnp.int32, S8, 1)
    base = 128 * first
    d[...] = a[0:128, 0:128]

    @pl.loop(0, 2)
    def _(p):
        blocks = chol_inv_128([d[8 * i : 8 * i + 8, :] for i in range(16)], sub, lane, rows)
        for i, block in enumerate(blocks):
            d[8 * i : 8 * i + 8, :] = block
        for q in range(2):

            @pl.when(p == q)
            def _():
                lo, hi = 128 * q, 128 * (q + 1)
                glo, ghi = base + lo, base + hi
                linv = d[...]
                if ghi < LEAD:
                    up = mm(linv, a[lo:hi, hi:])
                    left = a[hi:, hi:] - mtm(up, up)
                    a[hi:, hi:] = left
                    d[...] = left[:128, :128]
                o_ref[glo:ghi, glo:ghi] = linv
                if glo > 0:
                    o_ref[glo:ghi, :glo] = mm(linv, o_ref[glo:ghi, :glo])
                if ghi < LEAD:
                    o_ref[ghi:, :ghi] = o_ref[ghi:, :ghi] - mtm(up, o_ref[glo:ghi, :ghi])


def first_kernel(own, other, o_ref, left_ref, token, a, d, rows):
    core = lax.axis_index("col")
    a[:, aligned(core, 256)] = own[...]
    a[:, aligned(1 - core, 256)] = other[...]
    o_ref[...] = jnp.zeros_like(o_ref)
    panels(0, d, a, o_ref, rows)
    left_ref[...] = a[256:, 256:]
    token[...] = jnp.zeros_like(token)


def second_kernel(half_ref, left_ref, head_ref, tail_ref, o, a, d, rows):
    o[...] = half_ref[...]
    a[...] = left_ref[...]
    panels(2, d, a, o, rows)
    head_ref[:LEAD, :], head_ref[LEAD:, :] = two(o[:, :256])
    tail_ref[:256, :], tail_ref[256:, :] = two(o[256:, 256:])


def place():
    core, row = lax.axis_index("col"), lax.axis_index("row")
    x, y, z = row & 3, (row >> 2) & 3, row >> 4
    gray = lambda at: (at >> 1) ^ (at & 1)
    first = gray(x) | ((y >> 1) << 1) | (gray(z) << 2)
    second = (x >> 1) | (gray(y) << 1) | ((z >> 1) << 2)
    return jnp.where(core == 1, first, second)


def product_kernel(masks, head_ref, tail_ref, *refs):
    parts, (out_ref, buf, sems) = refs[: len(masks)], refs[-3:]
    mine = place()
    offset = lax.axis_index("col") * 2048
    dot = lambda x, y: jnp.dot(x, y, preferred_element_type=F32)
    copies = []
    for i, (m, part) in enumerate(zip(masks, parts)):
        xh, xl = two(part[:256])
        both = dot(head_ref[...], xh)
        y = both[:LEAD] + (both[LEAD:] + dot(head_ref[:LEAD], xl))
        xh, xl = two(part[256:])
        both = dot(tail_ref[...], xh)
        low = y[256:] + (both[:256] + (both[256:] + dot(tail_ref[:256], xl)))
        column = offset + (mine ^ m) * 256
        for r, block in ((0, y[:256]), (256, low)):
            ids = column + lax.broadcasted_iota(jnp.int32, block.shape, 1)
            buf[i, r : r + 256, :] = jnp.where(ids >= r + lax.broadcasted_iota(jnp.int32, block.shape, 0), block, 0.0)
        copies.append(pltpu.make_async_copy(buf.at[i], out_ref.at[:, aligned(mine ^ m, 256)], sems.at[i]))
        copies[-1].start()
    for copy in copies:
        copy.wait()


def product(masks, inverse, parts, out=None):
    n = len(parts)
    hbm = pl.BlockSpec(memory_space=pl.ANY)
    more = () if out is None else (out,)
    return pl.pallas_call(
        functools.partial(product_kernel, masks),
        out_shape=vmem(LEAD, 2048),
        in_specs=[VMEM] * (2 + n) + [hbm] * len(more),
        out_specs=hbm,
        scratch_shapes=[pltpu.VMEM((n, LEAD, 256), F32), pltpu.SemaphoreType.DMA((n,))],
        input_output_aliases={2 + n: 0} if more else {},
        compiler_params=pltpu.CompilerParams(vmem_limit_bytes=24 << 20),
        cost_estimate=cost(n * 400_000_000, n << 20),
        name="product",
    )(*inverse, *parts, *more)


def cubes(kind):
    groups = {}
    for chip in range(64):
        for core in range(2):
            inside = outside = 0
            for axis, at in enumerate((chip % 4, chip // 4 % 4, chip // 16)):
                bits = (at // 2 ^ at % 2, at // 2)
                first = kind ^ core ^ (axis != 1)
                inside += bits[first] << axis
                outside += bits[1 - first] << axis
            groups.setdefault((core, outside), {})[inside] = chip * 2 + core
    return [[group[i] for i in range(8)] for _, group in sorted(groups.items())]


PLUS, MINUS = cubes(0), cubes(1)


def flip(mask):
    return [(group[i], group[i ^ mask]) for group in PLUS for i in range(8)]


def exchange(x, groups):
    return lax.all_to_all(x, ("row", "col"), 0, 0, axis_index_groups=groups)


def body(contributions, valid_rows):
    blocks, height, width = contributions.shape
    core = lax.axis_index("col")

    def across(x):
        return lax.ppermute(x, "col", [(0, 1), (1, 0)])

    def copies(x):
        return jnp.broadcast_to(x[None], (8, *x.shape))

    def swap(x, mask):
        return lax.ppermute(x, ("row", "col"), flip(mask))

    raw = contributions.reshape(blocks * height, width)
    other = across(raw[:, :LEAD])
    live = jnp.arange(height, dtype=jnp.int32)[:, None] < valid_rows[0]
    masked = jnp.where(live, raw, 0.0)
    lead = jnp.where(core == 0, masked[:, :LEAD], jnp.where(live, other, 0.0))
    packed = exchange(call(pack_kernel, vmem(8, 128, 768), (masked, lead), name="pack"), PLUS)
    scratch = (pltpu.VMEM((1024, LEAD), F32),)
    grams = call(gram_kernel, vmem(8, 128, 256), (packed.reshape(1024, 768),), 1 << 30, 4 << 20, scratch, name="gram", limit=24)
    mine = jnp.sum(exchange(grams, MINUS), axis=0)
    whole = exchange(copies(mine), MINUS)
    rest, square = whole[:, :64].reshape(LEAD, 256), whole[:, 64:].reshape(LEAD, 256)

    near = [swap(rest, mask) for mask in (1, 2, 4)]
    far = swap(rest, 7)
    out = (vmem(LEAD, LEAD), vmem(256, 256), vmem(1, 256))
    scratch = (pltpu.VMEM((LEAD, LEAD), F32), pltpu.VMEM((128, 128), F32), pltpu.VMEM((336, 128), F32))
    half, left, zero = call(first_kernel, out, (square, across(square)), 10**10, 2 << 20, scratch, name="first")
    scratch = (pltpu.VMEM((LEAD, LEAD), F32), pltpu.VMEM((256, 256), F32), pltpu.VMEM((128, 128), F32), pltpu.VMEM((336, 128), F32))
    out = (jax.ShapeDtypeStruct((2 * LEAD, 256), jnp.bfloat16), jax.ShapeDtypeStruct((LEAD, 256), jnp.bfloat16))
    inverse = call(second_kernel, out, (half, left), 10**10, 2 << 20, scratch, name="second")
    x, y, z = (block + zero for block in near)
    xy, yz, zx = swap(y, 1), swap(z, 2), swap(x, 4)
    done = product((0, 1, 2, 4, 7), inverse, (rest, *near, far))
    return product((3, 6, 5), inverse, (xy, yz, zx), done)


def solution(mesh):
    return jax.shard_map(
        body,
        mesh=mesh,
        in_specs=(P(("front", "row"), None, "col"), P(("front", "row"))),
        out_specs=P("front", "col"),
        check_vma=False,
    )
```

```python
import functools

import jax
import jax.numpy as jnp
from jax import lax
from jax.experimental import pallas as pl
from jax.experimental.pallas import tpu as pltpu
from jax.sharding import PartitionSpec as P

LEAD = 512
HI = lax.Precision.HIGHEST


S8 = (8, 128)
F32 = jnp.float32
LEFT = (((0,), (0,)), ((), ()))


def lb(x, c):
    return jnp.broadcast_to(x[:, c : c + 1], S8)


def sb(x, j):
    return jnp.broadcast_to(x[j : j + 1, :], S8)


def mm(x, y):
    return jnp.dot(x, y, precision=HI, preferred_element_type=F32)


def mtm(x, y):
    return lax.dot_general(x, y, LEFT, precision=HI, preferred_element_type=F32)


def chol_inv_128(V, sub, lane, u):
    V=list(V)
    E=[jnp.where(lane==sub+8*k,1.0,0.0) for k in range(16)]
    out=[]
    for k in range(16):
        X=V[k]
        u[8*k:8*k+8,:]=X
        R=[u[pl.ds(8*k+j,8,stride=0),:] for j in range(8)]
        for j in range(8): u[256+8*j:264+8*j,:]=lb(X,8*k+j)
        S=[[u[pl.ds(256+8*j+i,8,stride=0),:] if i>=j else None for j in range(8)] for i in range(8)]
        u[128+8*k:136+8*k,:]=E[k]
        F=[u[pl.ds(128+8*k+j,8,stride=0),:] for j in range(8)]
        l=[[None]*8 for _ in range(8)]
        inv=[None]*8
        if k<15:
            Y1=V[k+1]
            C=[lb(Y1,8*k+j) for j in range(8)]
            v1=Y1; e1=E[k+1]
        for j in range(0,8,2):
            a,b,c=S[j][j],S[j+1][j],S[j+1][j+1]
            det=a*c-b*b
            both=1.0/det
            inv[j]=1.0/a
            inv[j+1]=a*both
            l[j+1][j]=b*inv[j]
            S[j+1][j+1]=det*inv[j]
            p={i:S[i][j] for i in range(j+2,8)}
            q={i:S[i][j+1] for i in range(j+2,8)}
            r={}
            near={}
            for i in range(j+2,min(j+4,8)):
                for m in range(j+2,i+1):
                    n=(c*p[i])*p[m]-b*(p[i]*q[m]+q[i]*p[m])+(a*q[i])*q[m] if i!=m else (c*p[i])*p[i]-(b+b)*(p[i]*q[i])+(a*q[i])*q[i]
                    near[i,m]=S[i][m]-n*both
            for i in range(j+2,8):
                l[i][j]=p[i]*inv[j]
                r[i]=q[i]-l[i][j]*b
                l[i][j+1]=r[i]*inv[j+1]
                for m in range(j+2,i+1):
                    S[i][m]=near[i,m] if (i,m) in near else S[i][m]-l[i][j]*p[m]-l[i][j+1]*r[m]
            for t in (j,j+1):
                if k<15:
                    cc=C[t]*inv[t]
                    v1=v1-cc*R[t]
                    e1=e1-cc*F[t]
                    for i in range(t+1,8):
                        C[i]=C[i]-l[i][t]*C[t]
                for i in range(t+1,8):
                    R[i]=R[i]-l[i][t]*R[t]
                    F[i]=F[i]-l[i][t]*F[t]
        o=F[0]*lax.rsqrt(S[0][0])
        for j in range(1,8):
            o=jnp.where(sub==j,F[j]*lax.rsqrt(S[j][j]),o)
        out.append(o)
        if k<15:
            V[k+1]=v1; E[k+1]=e1
        if k<14:
            W=[R[j]*inv[j] for j in range(8)]
            H=[F[j]*inv[j] for j in range(8)]
            for i in range(7,0,-1):
                for j in range(i):
                    W[j]=W[j]-l[i][j]*W[i]
                    H[j]=H[j]-l[i][j]*H[i]
            for m in range(k+2,16):
                Y=V[m]; v=Y; e=E[m]
                for j in range(7,-1,-1):
                    c=lb(Y,8*k+j)
                    v=v-c*W[j]
                    e=e-c*H[j]
                V[m]=v; E[m]=e
    return out


def vmem(*shape):
    return jax.ShapeDtypeStruct(shape, F32)


VMEM = pl.BlockSpec(memory_space=pltpu.VMEM)


def cost(flops, nbytes):
    return pl.CostEstimate(flops=flops, bytes_accessed=nbytes, transcendentals=0)


def aligned(i, n):
    return pl.ds(pl.multiple_of(i * n, n), n)


def call(kernel, out, args, flops=0, nbytes=1 << 20, scratch=(), out_specs=None, name=None, limit=12):
    return pl.pallas_call(
        kernel,
        out_shape=out,
        in_specs=[VMEM] * len(args),
        out_specs=out_specs or jax.tree.map(lambda _: VMEM, out),
        scratch_shapes=list(scratch),
        compiler_params=pltpu.CompilerParams(vmem_limit_bytes=limit << 20),
        cost_estimate=cost(flops, nbytes),
        name=name,
    )(*args)


def two(x):
    high = x.astype(jnp.bfloat16)
    return high, (x - high.astype(F32)).astype(jnp.bfloat16)


def pack_kernel(x_ref, lead_ref, out):
    for p in range(8):
        out[p, :, :LEAD] = lead_ref[...]
        out[p, :, LEAD:] = x_ref[:, 256 * p : 256 * p + 256]


def gram_kernel(x_ref, out, right):
    right[:, :256] = x_ref[:, LEAD:]
    right[:, 256:] = x_ref[:, aligned(lax.axis_index("col"), 256)]
    dot = lambda x, y: lax.dot_general(x, y, LEFT, preferred_element_type=F32)
    xh, xl = two(x_ref[:, :LEAD])
    yh, yl = two(right[...])
    gram = dot(xh, yh) + ((dot(xl, yh) + dot(xh, yl)) + dot(xl, yl))
    for p in range(8):
        out[p, :64, :] = gram[64 * p : 64 * p + 64, :256]
        out[p, 64:, :] = gram[64 * p : 64 * p + 64, 256:]


def panels(first, d, a, o_ref, rows):
    sub = lax.broadcasted_iota(jnp.int32, S8, 0)
    lane = lax.broadcasted_iota(jnp.int32, S8, 1)
    base = 128 * first
    d[...] = a[0:128, 0:128]

    @pl.loop(0, 2)
    def _(p):
        blocks = chol_inv_128([d[8 * i : 8 * i + 8, :] for i in range(16)], sub, lane, rows)
        for i, block in enumerate(blocks):
            d[8 * i : 8 * i + 8, :] = block
        for q in range(2):

            @pl.when(p == q)
            def _():
                lo, hi = 128 * q, 128 * (q + 1)
                glo, ghi = base + lo, base + hi
                linv = d[...]
                if ghi < LEAD:
                    up = mm(linv, a[lo:hi, hi:])
                    left = a[hi:, hi:] - mtm(up, up)
                    a[hi:, hi:] = left
                    d[...] = left[:128, :128]
                o_ref[glo:ghi, glo:ghi] = linv
                if glo > 0:
                    o_ref[glo:ghi, :glo] = mm(linv, o_ref[glo:ghi, :glo])
                if ghi < LEAD:
                    o_ref[ghi:, :ghi] = o_ref[ghi:, :ghi] - mtm(up, o_ref[glo:ghi, :ghi])


def first_kernel(own, other, o_ref, left_ref, token, a, d, rows):
    core = lax.axis_index("col")
    a[:, aligned(core, 256)] = own[...]
    a[:, aligned(1 - core, 256)] = other[...]
    o_ref[...] = jnp.zeros_like(o_ref)
    panels(0, d, a, o_ref, rows)
    left_ref[...] = a[256:, 256:]
    token[...] = jnp.zeros_like(token)


def second_kernel(half_ref, left_ref, head_ref, tail_ref, o, a, d, rows):
    o[...] = half_ref[...]
    a[...] = left_ref[...]
    panels(2, d, a, o, rows)
    head_ref[:LEAD, :], head_ref[LEAD:, :] = two(o[:, :256])
    tail_ref[:256, :], tail_ref[256:, :] = two(o[256:, 256:])


def later_kernel(x_ref, after_ref, out):
    out[...] = x_ref[...]


def place():
    core, row = lax.axis_index("col"), lax.axis_index("row")
    x, y, z = row & 3, (row >> 2) & 3, row >> 4
    gray = lambda at: (at >> 1) ^ (at & 1)
    first = gray(x) | ((y >> 1) << 1) | (gray(z) << 2)
    second = (x >> 1) | (gray(y) << 1) | ((z >> 1) << 2)
    return jnp.where(core == 1, first, second)


def product_kernel(masks, head_ref, tail_ref, *refs):
    parts, (out_ref, buf, sems) = refs[: len(masks)], refs[-3:]
    mine = place()
    offset = lax.axis_index("col") * 2048
    dot = lambda x, y: jnp.dot(x, y, preferred_element_type=F32)
    copies = []
    for i, (m, part) in enumerate(zip(masks, parts)):
        xh, xl = two(part[:256])
        both = dot(head_ref[...], xh)
        y = both[:LEAD] + (both[LEAD:] + dot(head_ref[:LEAD], xl))
        xh, xl = two(part[256:])
        both = dot(tail_ref[...], xh)
        low = y[256:] + (both[:256] + (both[256:] + dot(tail_ref[:256], xl)))
        column = offset + (mine ^ m) * 256
        for r, block in ((0, y[:256]), (256, low)):
            ids = column + lax.broadcasted_iota(jnp.int32, block.shape, 1)
            buf[i, r : r + 256, :] = jnp.where(ids >= r + lax.broadcasted_iota(jnp.int32, block.shape, 0), block, 0.0)
        copies.append(pltpu.make_async_copy(buf.at[i], out_ref.at[:, aligned(mine ^ m, 256)], sems.at[i]))
        copies[-1].start()
    for copy in copies:
        copy.wait()


def product(masks, inverse, parts, out=None):
    n = len(parts)
    hbm = pl.BlockSpec(memory_space=pl.ANY)
    more = () if out is None else (out,)
    return pl.pallas_call(
        functools.partial(product_kernel, masks),
        out_shape=vmem(LEAD, 2048),
        in_specs=[VMEM] * (2 + n) + [hbm] * len(more),
        out_specs=hbm,
        scratch_shapes=[pltpu.VMEM((n, LEAD, 256), F32), pltpu.SemaphoreType.DMA((n,))],
        input_output_aliases={2 + n: 0} if more else {},
        compiler_params=pltpu.CompilerParams(vmem_limit_bytes=24 << 20),
        cost_estimate=cost(n * 400_000_000, n << 20),
        name="product",
    )(*inverse, *parts, *more)


def cubes(kind):
    groups = {}
    for chip in range(64):
        for core in range(2):
            inside = outside = 0
            for axis, at in enumerate((chip % 4, chip // 4 % 4, chip // 16)):
                bits = (at // 2 ^ at % 2, at // 2)
                first = kind ^ core ^ (axis != 1)
                inside += bits[first] << axis
                outside += bits[1 - first] << axis
            groups.setdefault((core, outside), {})[inside] = chip * 2 + core
    return [[group[i] for i in range(8)] for _, group in sorted(groups.items())]


PLUS, MINUS = cubes(0), cubes(1)


def flip(mask):
    return [(group[i], group[i ^ mask]) for group in PLUS for i in range(8)]


def exchange(x, groups):
    return lax.all_to_all(x, ("row", "col"), 0, 0, axis_index_groups=groups)


def body(contributions, valid_rows):
    blocks, height, width = contributions.shape
    core = lax.axis_index("col")

    def across(x):
        return lax.ppermute(x, "col", [(0, 1), (1, 0)])

    def copies(x):
        return jnp.broadcast_to(x[None], (8, *x.shape))

    def swap(x, mask):
        return lax.ppermute(x, ("row", "col"), flip(mask))

    raw = contributions.reshape(blocks * height, width)
    other = across(raw[:, :LEAD])
    live = jnp.arange(height, dtype=jnp.int32)[:, None] < valid_rows[0]
    masked = jnp.where(live, raw, 0.0)
    lead = jnp.where(core == 0, masked[:, :LEAD], jnp.where(live, other, 0.0))
    packed = exchange(call(pack_kernel, vmem(8, 128, 768), (masked, lead), name="pack"), PLUS)
    scratch = (pltpu.VMEM((1024, LEAD), F32),)
    grams = call(gram_kernel, vmem(8, 128, 256), (packed.reshape(1024, 768),), 1 << 30, 4 << 20, scratch, name="gram", limit=24)
    mine = jnp.sum(exchange(grams, MINUS), axis=0)
    whole = exchange(copies(mine), MINUS)
    rest, square = whole[:, :64].reshape(LEAD, 256), whole[:, 64:].reshape(LEAD, 256)

    other = across(square)
    near = [swap(rest, mask) for mask in (1, 2, 4)]
    far = swap(call(later_kernel, vmem(LEAD, 256), (rest, other), name="later"), 7)
    out = (vmem(LEAD, LEAD), vmem(256, 256), vmem(1, 256))
    scratch = (pltpu.VMEM((LEAD, LEAD), F32), pltpu.VMEM((128, 128), F32), pltpu.VMEM((336, 128), F32))
    half, left, zero = call(first_kernel, out, (square, other), 10**10, 2 << 20, scratch, name="first")
    scratch = (pltpu.VMEM((LEAD, LEAD), F32), pltpu.VMEM((256, 256), F32), pltpu.VMEM((128, 128), F32), pltpu.VMEM((336, 128), F32))
    out = (jax.ShapeDtypeStruct((2 * LEAD, 256), jnp.bfloat16), jax.ShapeDtypeStruct((LEAD, 256), jnp.bfloat16))
    inverse = call(second_kernel, out, (half, left), 10**10, 2 << 20, scratch, name="second")
    x, y, z = (block + zero for block in near)
    xy, yz, zx = swap(y, 1), swap(z, 2), swap(x, 4)
    done = product((0, 1, 2, 4, 7), inverse, (rest, *near, far))
    return product((3, 6, 5), inverse, (xy, yz, zx), done)


def solution(mesh):
    return jax.shard_map(
        body,
        mesh=mesh,
        in_specs=(P(("front", "row"), None, "col"), P(("front", "row"))),
        out_specs=P("front", "col"),
        check_vma=False,
    )
```

```python
import functools

import jax
import jax.numpy as jnp
from jax import lax
from jax.experimental import pallas as pl
from jax.experimental.pallas import tpu as pltpu
from jax.sharding import PartitionSpec as P

LEAD = 512
HI = lax.Precision.HIGHEST


S8 = (8, 128)
F32 = jnp.float32
LEFT = (((0,), (0,)), ((), ()))


def lb(x, c):
    return jnp.broadcast_to(x[:, c : c + 1], S8)


def sb(x, j):
    return jnp.broadcast_to(x[j : j + 1, :], S8)


def mm(x, y):
    return jnp.dot(x, y, precision=HI, preferred_element_type=F32)


def mtm(x, y):
    return lax.dot_general(x, y, LEFT, precision=HI, preferred_element_type=F32)


def chol_inv_128(V, sub, lane, u):
    V=list(V)
    E=[jnp.where(lane==sub+8*k,1.0,0.0) for k in range(16)]
    out=[]
    for k in range(16):
        X=V[k]
        u[8*k:8*k+8,:]=X
        R=[u[pl.ds(8*k+j,8,stride=0),:] for j in range(8)]
        for j in range(8): u[256+8*j:264+8*j,:]=lb(X,8*k+j)
        S=[[u[pl.ds(256+8*j+i,8,stride=0),:] if i>=j else None for j in range(8)] for i in range(8)]
        u[128+8*k:136+8*k,:]=E[k]
        F=[u[pl.ds(128+8*k+j,8,stride=0),:] for j in range(8)]
        l=[[None]*8 for _ in range(8)]
        inv=[None]*8
        if k<15:
            Y1=V[k+1]
            C=[lb(Y1,8*k+j) for j in range(8)]
            v1=Y1; e1=E[k+1]
        for j in range(0,8,2):
            a,b,c=S[j][j],S[j+1][j],S[j+1][j+1]
            det=a*c-b*b
            both=1.0/det
            inv[j]=1.0/a
            inv[j+1]=a*both
            l[j+1][j]=b*inv[j]
            S[j+1][j+1]=det*inv[j]
            p={i:S[i][j] for i in range(j+2,8)}
            q={i:S[i][j+1] for i in range(j+2,8)}
            r={}
            near={}
            for i in range(j+2,min(j+4,8)):
                for m in range(j+2,i+1):
                    n=(c*p[i])*p[m]-b*(p[i]*q[m]+q[i]*p[m])+(a*q[i])*q[m] if i!=m else (c*p[i])*p[i]-(b+b)*(p[i]*q[i])+(a*q[i])*q[i]
                    near[i,m]=S[i][m]-n*both
            for i in range(j+2,8):
                l[i][j]=p[i]*inv[j]
                r[i]=q[i]-l[i][j]*b
                l[i][j+1]=r[i]*inv[j+1]
                for m in range(j+2,i+1):
                    S[i][m]=near[i,m] if (i,m) in near else S[i][m]-l[i][j]*p[m]-l[i][j+1]*r[m]
            for t in (j,j+1):
                if k<15:
                    cc=C[t]*inv[t]
                    v1=v1-cc*R[t]
                    e1=e1-cc*F[t]
                    for i in range(t+1,8):
                        C[i]=C[i]-l[i][t]*C[t]
                for i in range(t+1,8):
                    R[i]=R[i]-l[i][t]*R[t]
                    F[i]=F[i]-l[i][t]*F[t]
        o=F[0]*lax.rsqrt(S[0][0])
        for j in range(1,8):
            o=jnp.where(sub==j,F[j]*lax.rsqrt(S[j][j]),o)
        out.append(o)
        if k<15:
            V[k+1]=v1; E[k+1]=e1
        if k<14:
            W=[R[j]*inv[j] for j in range(8)]
            H=[F[j]*inv[j] for j in range(8)]
            for i in range(7,0,-1):
                for j in range(i):
                    W[j]=W[j]-l[i][j]*W[i]
                    H[j]=H[j]-l[i][j]*H[i]
            for m in range(k+2,16):
                Y=V[m]; v=Y; e=E[m]
                for j in range(7,-1,-1):
                    c=lb(Y,8*k+j)
                    v=v-c*W[j]
                    e=e-c*H[j]
                V[m]=v; E[m]=e
    return out


def vmem(*shape):
    return jax.ShapeDtypeStruct(shape, F32)


VMEM = pl.BlockSpec(memory_space=pltpu.VMEM)


def cost(flops, nbytes):
    return pl.CostEstimate(flops=flops, bytes_accessed=nbytes, transcendentals=0)


def aligned(i, n):
    return pl.ds(pl.multiple_of(i * n, n), n)


def call(kernel, out, args, flops=0, nbytes=1 << 20, scratch=(), out_specs=None, name=None, limit=12):
    return pl.pallas_call(
        kernel,
        out_shape=out,
        in_specs=[VMEM] * len(args),
        out_specs=out_specs or jax.tree.map(lambda _: VMEM, out),
        scratch_shapes=list(scratch),
        compiler_params=pltpu.CompilerParams(vmem_limit_bytes=limit << 20),
        cost_estimate=cost(flops, nbytes),
        name=name,
    )(*args)


def two(x):
    high = x.astype(jnp.bfloat16)
    return high, (x - high.astype(F32)).astype(jnp.bfloat16)


def pack_kernel(x_ref, lead_ref, out):
    for p in range(8):
        out[p, :, :LEAD] = lead_ref[...]
        out[p, :, LEAD:] = x_ref[:, 256 * p : 256 * p + 256]


def gram_kernel(x_ref, out, right):
    right[:, :256] = x_ref[:, LEAD:]
    right[:, 256:] = x_ref[:, aligned(lax.axis_index("col"), 256)]
    dot = lambda x, y: lax.dot_general(x, y, LEFT, preferred_element_type=F32)
    xh, xl = two(x_ref[:, :LEAD])
    yh, yl = two(right[...])
    gram = dot(xh, yh) + ((dot(xl, yh) + dot(xh, yl)) + dot(xl, yl))
    for p in range(8):
        out[p, :64, :] = gram[64 * p : 64 * p + 64, :256]
        out[p, 64:, :] = gram[64 * p : 64 * p + 64, 256:]


def panels(first, d, a, o_ref, rows):
    sub = lax.broadcasted_iota(jnp.int32, S8, 0)
    lane = lax.broadcasted_iota(jnp.int32, S8, 1)
    base = 128 * first
    d[...] = a[0:128, 0:128]

    @pl.loop(0, 2)
    def _(p):
        blocks = chol_inv_128([d[8 * i : 8 * i + 8, :] for i in range(16)], sub, lane, rows)
        for i, block in enumerate(blocks):
            d[8 * i : 8 * i + 8, :] = block
        for q in range(2):

            @pl.when(p == q)
            def _():
                lo, hi = 128 * q, 128 * (q + 1)
                glo, ghi = base + lo, base + hi
                linv = d[...]
                if ghi < LEAD:
                    up = mm(linv, a[lo:hi, hi:])
                    left = a[hi:, hi:] - mtm(up, up)
                    a[hi:, hi:] = left
                    d[...] = left[:128, :128]
                o_ref[glo:ghi, glo:ghi] = linv
                if glo > 0:
                    o_ref[glo:ghi, :glo] = mm(linv, o_ref[glo:ghi, :glo])
                if ghi < LEAD:
                    o_ref[ghi:, :ghi] = o_ref[ghi:, :ghi] - mtm(up, o_ref[glo:ghi, :ghi])


def first_kernel(own, other, o_ref, left_ref, t0, t1, t2, a, d, rows):
    core = lax.axis_index("col")
    a[:, aligned(core, 256)] = own[...]
    a[:, aligned(1 - core, 256)] = other[...]
    o_ref[...] = jnp.zeros_like(o_ref)
    panels(0, d, a, o_ref, rows)
    left_ref[...] = a[256:, 256:]
    for token in (t0, t1, t2):
        token[...] = jnp.zeros_like(token)


def second_kernel(half_ref, left_ref, head_ref, tail_ref, o, a, d, rows):
    o[...] = half_ref[...]
    a[...] = left_ref[...]
    panels(2, d, a, o, rows)
    head_ref[:LEAD, :], head_ref[LEAD:, :] = two(o[:, :256])
    tail_ref[:256, :], tail_ref[256:, :] = two(o[256:, 256:])


def place():
    core, row = lax.axis_index("col"), lax.axis_index("row")
    x, y, z = row & 3, (row >> 2) & 3, row >> 4
    gray = lambda at: (at >> 1) ^ (at & 1)
    first = gray(x) | ((y >> 1) << 1) | (gray(z) << 2)
    second = (x >> 1) | (gray(y) << 1) | ((z >> 1) << 2)
    return jnp.where(core == 1, first, second)


def product_kernel(masks, head_ref, tail_ref, *refs):
    parts, (out_ref, buf, sems) = refs[: len(masks)], refs[-3:]
    mine = place()
    offset = lax.axis_index("col") * 2048
    dot = lambda x, y: jnp.dot(x, y, preferred_element_type=F32)
    copies = []
    for i, (m, part) in enumerate(zip(masks, parts)):
        xh, xl = two(part[:256])
        both = dot(head_ref[...], xh)
        y = both[:LEAD] + (both[LEAD:] + dot(head_ref[:LEAD], xl))
        xh, xl = two(part[256:])
        both = dot(tail_ref[...], xh)
        low = y[256:] + (both[:256] + (both[256:] + dot(tail_ref[:256], xl)))
        column = offset + (mine ^ m) * 256
        for r, block in ((0, y[:256]), (256, low)):
            ids = column + lax.broadcasted_iota(jnp.int32, block.shape, 1)
            buf[i, r : r + 256, :] = jnp.where(ids >= r + lax.broadcasted_iota(jnp.int32, block.shape, 0), block, 0.0)
        copies.append(pltpu.make_async_copy(buf.at[i], out_ref.at[:, aligned(mine ^ m, 256)], sems.at[i]))
        copies[-1].start()
    for copy in copies:
        copy.wait()


def product(masks, inverse, parts, out=None):
    n = len(parts)
    hbm = pl.BlockSpec(memory_space=pl.ANY)
    more = () if out is None else (out,)
    return pl.pallas_call(
        functools.partial(product_kernel, masks),
        out_shape=vmem(LEAD, 2048),
        in_specs=[VMEM] * (2 + n) + [hbm] * len(more),
        out_specs=hbm,
        scratch_shapes=[pltpu.VMEM((n, LEAD, 256), F32), pltpu.SemaphoreType.DMA((n,))],
        input_output_aliases={2 + n: 0} if more else {},
        compiler_params=pltpu.CompilerParams(vmem_limit_bytes=24 << 20),
        cost_estimate=cost(n * 400_000_000, n << 20),
        name="product",
    )(*inverse, *parts, *more)


def cubes(kind):
    groups = {}
    for chip in range(64):
        for core in range(2):
            inside = outside = 0
            for axis, at in enumerate((chip % 4, chip // 4 % 4, chip // 16)):
                bits = (at // 2 ^ at % 2, at // 2)
                first = kind ^ core ^ (axis != 1)
                inside += bits[first] << axis
                outside += bits[1 - first] << axis
            groups.setdefault((core, outside), {})[inside] = chip * 2 + core
    return [[group[i] for i in range(8)] for _, group in sorted(groups.items())]


PLUS, MINUS = cubes(0), cubes(1)


def flip(mask):
    return [(group[i], group[i ^ mask]) for group in PLUS for i in range(8)]


def exchange(x, groups):
    return lax.all_to_all(x, ("row", "col"), 0, 0, axis_index_groups=groups)


def body(contributions, valid_rows):
    blocks, height, width = contributions.shape
    core = lax.axis_index("col")

    def across(x):
        return lax.ppermute(x, "col", [(0, 1), (1, 0)])

    def copies(x):
        return jnp.broadcast_to(x[None], (8, *x.shape))

    def swap(x, mask):
        return lax.ppermute(x, ("row", "col"), flip(mask))

    raw = contributions.reshape(blocks * height, width)
    other = across(raw[:, :LEAD])
    live = jnp.arange(height, dtype=jnp.int32)[:, None] < valid_rows[0]
    masked = jnp.where(live, raw, 0.0)
    lead = jnp.where(core == 0, masked[:, :LEAD], jnp.where(live, other, 0.0))
    packed = exchange(call(pack_kernel, vmem(8, 128, 768), (masked, lead), name="pack"), PLUS)
    scratch = (pltpu.VMEM((1024, LEAD), F32),)
    grams = call(gram_kernel, vmem(8, 128, 256), (packed.reshape(1024, 768),), 1 << 30, 4 << 20, scratch, name="gram", limit=24)
    mine = jnp.sum(exchange(grams, MINUS), axis=0)
    whole = exchange(copies(mine), MINUS)
    rest, square = whole[:, :64].reshape(LEAD, 256), whole[:, 64:].reshape(LEAD, 256)

    near = [swap(rest, mask) for mask in (1, 2, 4)]
    far = swap(rest, 7)
    out = (vmem(LEAD, LEAD), vmem(256, 256), *[vmem(1, 256)] * 3)
    scratch = (pltpu.VMEM((LEAD, LEAD), F32), pltpu.VMEM((128, 128), F32), pltpu.VMEM((336, 128), F32))
    half, left, *zeros = call(first_kernel, out, (square, across(square)), 10**10, 2 << 20, scratch, name="first")
    scratch = (pltpu.VMEM((LEAD, LEAD), F32), pltpu.VMEM((256, 256), F32), pltpu.VMEM((128, 128), F32), pltpu.VMEM((336, 128), F32))
    out = (jax.ShapeDtypeStruct((2 * LEAD, 256), jnp.bfloat16), jax.ShapeDtypeStruct((LEAD, 256), jnp.bfloat16))
    inverse = call(second_kernel, out, (half, left), 10**10, 2 << 20, scratch, name="second")
    x, y, z = (block + zero for block, zero in zip(near, zeros))
    xy, yz, zx = swap(y, 1), swap(z, 2), swap(x, 4)
    done = product((0, 1, 2, 4, 7), inverse, (rest, *near, far))
    return product((3, 6, 5), inverse, (xy, yz, zx), done)


def solution(mesh):
    return jax.shard_map(
        body,
        mesh=mesh,
        in_specs=(P(("front", "row"), None, "col"), P(("front", "row"))),
        out_specs=P("front", "col"),
        check_vma=False,
    )
```

```python
import functools

import jax
import jax.numpy as jnp
from jax import lax
from jax.experimental import pallas as pl
from jax.experimental.pallas import tpu as pltpu
from jax.sharding import PartitionSpec as P

LEAD = 512
HI = lax.Precision.HIGHEST


S8 = (8, 128)
F32 = jnp.float32
LEFT = (((0,), (0,)), ((), ()))


def lb(x, c):
    return jnp.broadcast_to(x[:, c : c + 1], S8)


def sb(x, j):
    return jnp.broadcast_to(x[j : j + 1, :], S8)


def mm(x, y):
    return jnp.dot(x, y, precision=HI, preferred_element_type=F32)


def mtm(x, y):
    return lax.dot_general(x, y, LEFT, precision=HI, preferred_element_type=F32)


def chol_inv_128(V, sub, lane, u):
    V=list(V)
    E=[jnp.where(lane==sub+8*k,1.0,0.0) for k in range(16)]
    out=[]
    for k in range(16):
        X=V[k]
        u[8*k:8*k+8,:]=X
        R=[u[pl.ds(8*k+j,8,stride=0),:] for j in range(8)]
        for j in range(8): u[256+64*k+8*j:264+64*k+8*j,:]=lb(X,8*k+j)
        S=[[u[pl.ds(256+64*k+8*j+i,8,stride=0),:] if i>=j else None for j in range(8)] for i in range(8)]
        u[128+8*k:136+8*k,:]=E[k]
        F=[u[pl.ds(128+8*k+j,8,stride=0),:] for j in range(8)]
        l=[[None]*8 for _ in range(8)]
        inv=[None]*8
        if k<15:
            Y1=V[k+1]
            C=[lb(Y1,8*k+j) for j in range(8)]
            v1=Y1; e1=E[k+1]
        for j in range(0,8,2):
            a,b,c=S[j][j],S[j+1][j],S[j+1][j+1]
            det=a*c-b*b
            both=1.0/det
            inv[j]=1.0/a
            inv[j+1]=a*both
            l[j+1][j]=b*inv[j]
            S[j+1][j+1]=det*inv[j]
            p={i:S[i][j] for i in range(j+2,8)}
            q={i:S[i][j+1] for i in range(j+2,8)}
            r={}
            near={}
            for i in range(j+2,min(j+4,8)):
                for m in range(j+2,i+1):
                    n=(c*p[i])*p[m]-b*(p[i]*q[m]+q[i]*p[m])+(a*q[i])*q[m] if i!=m else (c*p[i])*p[i]-(b+b)*(p[i]*q[i])+(a*q[i])*q[i]
                    near[i,m]=S[i][m]-n*both
            for i in range(j+2,8):
                l[i][j]=p[i]*inv[j]
                r[i]=q[i]-l[i][j]*b
                l[i][j+1]=r[i]*inv[j+1]
                for m in range(j+2,i+1):
                    S[i][m]=near[i,m] if (i,m) in near else S[i][m]-l[i][j]*p[m]-l[i][j+1]*r[m]
            for t in (j,j+1):
                if k<15:
                    v1=v1-C[t]*(R[t]*inv[t])
                    e1=e1-C[t]*(F[t]*inv[t])
                    for i in range(t+1,8):
                        C[i]=C[i]-l[i][t]*C[t]
                for i in range(t+1,8):
                    R[i]=R[i]-l[i][t]*R[t]
                    F[i]=F[i]-l[i][t]*F[t]
        o=F[0]*lax.rsqrt(S[0][0])
        for j in range(1,8):
            o=jnp.where(sub==j,F[j]*lax.rsqrt(S[j][j]),o)
        out.append(o)
        if k<15:
            V[k+1]=v1; E[k+1]=e1
        if k<14:
            W=[R[j]*inv[j] for j in range(8)]
            H=[F[j]*inv[j] for j in range(8)]
            for i in range(7,0,-1):
                for j in range(i):
                    W[j]=W[j]-l[i][j]*W[i]
                    H[j]=H[j]-l[i][j]*H[i]
            for m in range(k+2,16):
                Y=V[m]; v=Y; e=E[m]
                for j in range(7,-1,-1):
                    c=lb(Y,8*k+j)
                    v=v-c*W[j]
                    e=e-c*H[j]
                V[m]=v; E[m]=e
    return out


def vmem(*shape):
    return jax.ShapeDtypeStruct(shape, F32)


VMEM = pl.BlockSpec(memory_space=pltpu.VMEM)


def cost(flops, nbytes):
    return pl.CostEstimate(flops=flops, bytes_accessed=nbytes, transcendentals=0)


def aligned(i, n):
    return pl.ds(pl.multiple_of(i * n, n), n)


def call(kernel, out, args, flops=0, nbytes=1 << 20, scratch=(), out_specs=None, name=None, limit=12):
    return pl.pallas_call(
        kernel,
        out_shape=out,
        in_specs=[VMEM] * len(args),
        out_specs=out_specs or jax.tree.map(lambda _: VMEM, out),
        scratch_shapes=list(scratch),
        compiler_params=pltpu.CompilerParams(vmem_limit_bytes=limit << 20),
        cost_estimate=cost(flops, nbytes),
        name=name,
    )(*args)


def two(x):
    high = x.astype(jnp.bfloat16)
    return high, (x - high.astype(F32)).astype(jnp.bfloat16)


def pack_kernel(x_ref, lead_ref, out):
    for p in range(8):
        out[p, :, :LEAD] = lead_ref[...]
        out[p, :, LEAD:] = x_ref[:, 256 * p : 256 * p + 256]


def gram_kernel(x_ref, out, right):
    right[:, :256] = x_ref[:, LEAD:]
    right[:, 256:] = x_ref[:, aligned(lax.axis_index("col"), 256)]
    dot = lambda x, y: lax.dot_general(x, y, LEFT, preferred_element_type=F32)
    xh, xl = two(x_ref[:, :LEAD])
    yh, yl = two(right[...])
    gram = dot(xh, yh) + ((dot(xl, yh) + dot(xh, yl)) + dot(xl, yl))
    for p in range(8):
        out[p, :64, :] = gram[64 * p : 64 * p + 64, :256]
        out[p, 64:, :] = gram[64 * p : 64 * p + 64, 256:]


def panels(first, d, a, o_ref, rows):
    sub = lax.broadcasted_iota(jnp.int32, S8, 0)
    lane = lax.broadcasted_iota(jnp.int32, S8, 1)
    base = 128 * first
    d[...] = a[0:128, 0:128]

    @pl.loop(0, 2)
    def _(p):
        blocks = chol_inv_128([d[8 * i : 8 * i + 8, :] for i in range(16)], sub, lane, rows)
        for i, block in enumerate(blocks):
            d[8 * i : 8 * i + 8, :] = block
        for q in range(2):

            @pl.when(p == q)
            def _():
                lo, hi = 128 * q, 128 * (q + 1)
                glo, ghi = base + lo, base + hi
                linv = d[...]
                if ghi < LEAD:
                    up = mm(linv, a[lo:hi, hi:])
                    left = a[hi:, hi:] - mtm(up, up)
                    a[hi:, hi:] = left
                    d[...] = left[:128, :128]
                o_ref[glo:ghi, glo:ghi] = linv
                if glo > 0:
                    o_ref[glo:ghi, :glo] = mm(linv, o_ref[glo:ghi, :glo])
                if ghi < LEAD:
                    o_ref[ghi:, :ghi] = o_ref[ghi:, :ghi] - mtm(up, o_ref[glo:ghi, :ghi])


def first_kernel(own, other, o_ref, left_ref, token, a, d, rows):
    core = lax.axis_index("col")
    a[:, aligned(core, 256)] = own[...]
    a[:, aligned(1 - core, 256)] = other[...]
    o_ref[...] = jnp.zeros_like(o_ref)
    panels(0, d, a, o_ref, rows)
    left_ref[...] = a[256:, 256:]
    token[...] = jnp.zeros_like(token)


def second_kernel(half_ref, left_ref, head_ref, tail_ref, o, a, d, rows):
    o[...] = half_ref[...]
    a[...] = left_ref[...]
    panels(2, d, a, o, rows)
    head_ref[:LEAD, :], head_ref[LEAD:, :] = two(o[:, :256])
    tail_ref[:256, :], tail_ref[256:, :] = two(o[256:, 256:])


def place():
    core, row = lax.axis_index("col"), lax.axis_index("row")
    x, y, z = row & 3, (row >> 2) & 3, row >> 4
    gray = lambda at: (at >> 1) ^ (at & 1)
    first = gray(x) | ((y >> 1) << 1) | (gray(z) << 2)
    second = (x >> 1) | (gray(y) << 1) | ((z >> 1) << 2)
    return jnp.where(core == 1, first, second)


def product_kernel(masks, head_ref, tail_ref, *refs):
    parts, (out_ref, buf, sems) = refs[: len(masks)], refs[-3:]
    mine = place()
    offset = lax.axis_index("col") * 2048
    dot = lambda x, y: jnp.dot(x, y, preferred_element_type=F32)
    copies = []
    for i, (m, part) in enumerate(zip(masks, parts)):
        xh, xl = two(part[:256])
        both = dot(head_ref[...], xh)
        y = both[:LEAD] + (both[LEAD:] + dot(head_ref[:LEAD], xl))
        xh, xl = two(part[256:])
        both = dot(tail_ref[...], xh)
        low = y[256:] + (both[:256] + (both[256:] + dot(tail_ref[:256], xl)))
        column = offset + (mine ^ m) * 256
        for r, block in ((0, y[:256]), (256, low)):
            ids = column + lax.broadcasted_iota(jnp.int32, block.shape, 1)
            buf[i, r : r + 256, :] = jnp.where(ids >= r + lax.broadcasted_iota(jnp.int32, block.shape, 0), block, 0.0)
        copies.append(pltpu.make_async_copy(buf.at[i], out_ref.at[:, aligned(mine ^ m, 256)], sems.at[i]))
        copies[-1].start()
    for copy in copies:
        copy.wait()


def product(masks, inverse, parts, out=None):
    n = len(parts)
    hbm = pl.BlockSpec(memory_space=pl.ANY)
    more = () if out is None else (out,)
    return pl.pallas_call(
        functools.partial(product_kernel, masks),
        out_shape=vmem(LEAD, 2048),
        in_specs=[VMEM] * (2 + n) + [hbm] * len(more),
        out_specs=hbm,
        scratch_shapes=[pltpu.VMEM((n, LEAD, 256), F32), pltpu.SemaphoreType.DMA((n,))],
        input_output_aliases={2 + n: 0} if more else {},
        compiler_params=pltpu.CompilerParams(vmem_limit_bytes=24 << 20),
        cost_estimate=cost(n * 400_000_000, n << 20),
        name="product",
    )(*inverse, *parts, *more)


def cubes(kind):
    groups = {}
    for chip in range(64):
        for core in range(2):
            inside = outside = 0
            for axis, at in enumerate((chip % 4, chip // 4 % 4, chip // 16)):
                bits = (at // 2 ^ at % 2, at // 2)
                first = kind ^ core ^ (axis != 1)
                inside += bits[first] << axis
                outside += bits[1 - first] << axis
            groups.setdefault((core, outside), {})[inside] = chip * 2 + core
    return [[group[i] for i in range(8)] for _, group in sorted(groups.items())]


PLUS, MINUS = cubes(0), cubes(1)


def flip(mask):
    return [(group[i], group[i ^ mask]) for group in PLUS for i in range(8)]


def exchange(x, groups):
    return lax.all_to_all(x, ("row", "col"), 0, 0, axis_index_groups=groups)


def body(contributions, valid_rows):
    blocks, height, width = contributions.shape
    core = lax.axis_index("col")

    def across(x):
        return lax.ppermute(x, "col", [(0, 1), (1, 0)])

    def copies(x):
        return jnp.broadcast_to(x[None], (8, *x.shape))

    def swap(x, mask):
        return lax.ppermute(x, ("row", "col"), flip(mask))

    raw = contributions.reshape(blocks * height, width)
    other = across(raw[:, :LEAD])
    live = jnp.arange(height, dtype=jnp.int32)[:, None] < valid_rows[0]
    masked = jnp.where(live, raw, 0.0)
    lead = jnp.where(core == 0, masked[:, :LEAD], jnp.where(live, other, 0.0))
    packed = exchange(call(pack_kernel, vmem(8, 128, 768), (masked, lead), name="pack"), PLUS)
    scratch = (pltpu.VMEM((1024, LEAD), F32),)
    grams = call(gram_kernel, vmem(8, 128, 256), (packed.reshape(1024, 768),), 1 << 30, 4 << 20, scratch, name="gram", limit=24)
    mine = jnp.sum(exchange(grams, MINUS), axis=0)
    whole = exchange(copies(mine), MINUS)
    rest, square = whole[:, :64].reshape(LEAD, 256), whole[:, 64:].reshape(LEAD, 256)

    near = [swap(rest, mask) for mask in (1, 2, 4)]
    far = swap(rest, 7)
    out = (vmem(LEAD, LEAD), vmem(256, 256), vmem(1, 256))
    scratch = (pltpu.VMEM((LEAD, LEAD), F32), pltpu.VMEM((128, 128), F32), pltpu.VMEM((1288, 128), F32))
    half, left, zero = call(first_kernel, out, (square, across(square)), 10**10, 2 << 20, scratch, name="first")
    scratch = (pltpu.VMEM((LEAD, LEAD), F32), pltpu.VMEM((256, 256), F32), pltpu.VMEM((128, 128), F32), pltpu.VMEM((1288, 128), F32))
    out = (jax.ShapeDtypeStruct((2 * LEAD, 256), jnp.bfloat16), jax.ShapeDtypeStruct((LEAD, 256), jnp.bfloat16))
    inverse = call(second_kernel, out, (half, left), 10**10, 2 << 20, scratch, name="second")
    x, y, z = (block + zero for block in near)
    xy, yz, zx = swap(y, 1), swap(z, 2), swap(x, 4)
    done = product((0, 1, 2, 4, 7), inverse, (rest, *near, far))
    return product((3, 6, 5), inverse, (xy, yz, zx), done)


def solution(mesh):
    return jax.shard_map(
        body,
        mesh=mesh,
        in_specs=(P(("front", "row"), None, "col"), P(("front", "row"))),
        out_specs=P("front", "col"),
        check_vma=False,
    )
```
